32 devices in a mesh: parts: 2 (over y), rep: 4 (over x, core), tp: 4 (over z).
Axes of the slice: x: 2, y: 2, z: 4, core: 2. Of those that a mesh axis runs over, the one named last changes fastest.
Arguments:
- queries: bfloat16 [512, 4, 4096], P(('parts', 'rep', 'tp')), parts along dimension 0, may hold values from -16 to 16
- cached_key_store: bfloat16 [512, 4, 128, 128], P(('parts', 'rep', 'tp')), parts along dimension 0, may hold values from -6 to 6
- cached_value_store: bfloat16 [512, 4, 128, 128], P(('parts', 'rep', 'tp')), parts along dimension 0, may hold values from -6 to 6
- decode_step_keys: bfloat16 [512, 4, 4, 128], P(('parts', 'rep', 'tp')), parts along dimension 0, may hold values from -6 to 6
- decode_step_values: bfloat16 [512, 4, 4, 128], P(('parts', 'rep', 'tp')), parts along dimension 0, may hold values from -6 to 6
- request_cache_length: int32 [512], P(('parts', 'rep', 'tp')), parts along dimension 0, may hold values from 2 to 128, as said below
- output_projection_weight: bfloat16 [4096, 4096], P('tp'), may hold values from -0.09375 to 0.09375
- adapter_down_weight: bfloat16 [8, 4096, 128], P('rep', 'tp'), may hold values from -0.09375 to 0.09375
- adapter_up_weight: bfloat16 [8, 128, 4096], P('rep', None, 'tp'), may hold values from -0.5 to 0.5
- adapter_store_slot: int32 [8], replicated, may hold values from 0 to 7, as said below
- adapter_ranks: int32 [8], replicated, may hold values from 8 to 128, as said below
- request_block_adapter: int32 [16], P('rep'), may hold values from 0 to 7, as said below
Outputs:
- attn_proj: bfloat16 [512, 4, 4096], P(('parts', 'rep'), None, 'tp'), parts along dimension 0
The draws below stay inside these ranges and needn't reach their ends.
There are 2 independent parts, one for each index of `parts`. The reference program is written for one: setup_inputs(seed, part) draws one part's arguments, and reference() takes and returns one part's arrays. A program takes and returns all parts, laid end to end along the dimension named above; an argument that names none is the same for every part. Nothing has to cross between parts.
Inputs may be any that keep to these rules, and one draw needn't show every extreme that they name: `request_cache_length`: some request has exactly 128 live positions. A permutation; adapter a lives at index adapter_store_slot[a] of adapter_down_weight and adapter_up_weight, on replica adapter_store_slot[a] // 2. `adapter_ranks`: 128 divided by a power of two; both ends occur. `request_block_adapter`: the 4 blocks of one replica use adapters that live on 4 different replicas; one replica holds an adapter of a block from every replica.
All inputs are finite; a program needn't handle non-finite values.
Results may differ from the reference program's by a relative error of at most 0.012.
Values may be sent and summed in bfloat16 or wider, within the bound.
No kernel may reach another device: no remote copies, remote signals or barrier semaphores. Data moves between devices by JAX's collectives and lax.ppermute only.
A program may use at most 64 MiB of HBM per device.

```python
import math
import jax
import jax.numpy as jnp
from jax import lax

MODEL_WIDTH = 4096
QUERY_HEADS = 32
KV_HEADS = 4
HEAD_SIZE = 128
MAXIMUM_RANK = 128
STEPS = 4
L = 128
NBLK_REP = 4
AD_REP = 2
REQS = 256
ADAPTER_COUNT = 8
N_TP = 4


def draw_queries(key, part):
    key = jax.random.fold_in(key, 3)
    drawn = jnp.clip(1.5 * jax.random.normal(key, (REQS, STEPS, QUERY_HEADS * HEAD_SIZE), jnp.float32), -10.0, 10.0)
    return drawn.astype(jnp.bfloat16)


def draw_cached_key_store(key, part):
    key = jax.random.fold_in(key, 5)
    shape_all = (REQS, KV_HEADS, L, HEAD_SIZE)
    drawn = jnp.clip(jax.random.normal(key, shape_all, jnp.float32), -6.0, 6.0)
    return drawn.astype(jnp.bfloat16)


def draw_request_cache_length(key, part):
    key = jax.random.fold_in(key, 7)
    first_key, second_key = jax.random.split(key)
    lengths = jax.random.randint(first_key, (REQS,), 2, L + 1)
    longest = jax.random.randint(second_key, (), 0, REQS)
    return jnp.where(jnp.arange(REQS) == longest, L, lengths).astype(jnp.int32)


def placement_draw(key):
    perm_key, hot_key, order_key, shuffle_key, local_key = jax.random.split(key, 5)
    rep_count = ADAPTER_COUNT // AD_REP
    slot_of = jax.random.permutation(perm_key, ADAPTER_COUNT)
    hottest = jax.random.randint(hot_key, (), 0, rep_count)

    def sender_homes(sender_key, mixing_key):
        order = jax.random.permutation(sender_key, rep_count)
        position = jnp.argsort(order)
        position = jnp.where(jnp.arange(rep_count) == hottest, -1, position)
        homes = jnp.argsort(position)[:NBLK_REP]
        return homes[jax.random.permutation(mixing_key, NBLK_REP)]
    homes_all = jax.vmap(sender_homes)(jax.random.split(order_key, rep_count), jax.random.split(shuffle_key, rep_count))
    local_pick = jax.random.randint(local_key, (rep_count, NBLK_REP), 0, AD_REP)
    slots_used = (homes_all * AD_REP + local_pick).reshape(-1)
    adapter_at = jnp.argsort(slot_of)
    return (slot_of.astype(jnp.int32), adapter_at[slots_used].astype(jnp.int32))


def draw_adapter_store_slot(key, part):
    slots_drawn, blocks_drawn = placement_draw(key)
    return slots_drawn


def draw_request_block_adapter(key, part):
    slots_drawn, blocks_drawn = placement_draw(key)
    return blocks_drawn


def draw_adapter_ranks(key, part):
    key = jax.random.fold_in(key, 13)
    power_key, high_key, low_key = jax.random.split(key, 3)
    powers = jax.random.randint(power_key, (ADAPTER_COUNT,), 0, 5)
    ranks = MAXIMUM_RANK // jnp.left_shift(1, powers)
    highest = jax.random.randint(high_key, (), 0, ADAPTER_COUNT)
    lowest = (highest + 1 + jax.random.randint(low_key, (), 0, ADAPTER_COUNT - 1)) % ADAPTER_COUNT
    positions = jnp.arange(ADAPTER_COUNT)
    ranks = jnp.where(positions == highest, MAXIMUM_RANK, ranks)
    ranks = jnp.where(positions == lowest, MAXIMUM_RANK // 16, ranks)
    return ranks.astype(jnp.int32)


def level_of(key, extent, pieces, smallest, largest):
    def one(dim, blocks):
        draws = jax.random.uniform(jax.random.fold_in(jax.random.fold_in(key, 6), dim), (blocks,), jnp.float32, smallest / len(pieces), largest / len(pieces))
        return jnp.repeat(jnp.exp(draws), extent[dim] // blocks).reshape((-1,) + (1,) * (len(extent) - dim - 1))

    factor_of = one(*pieces[0])
    for cut in pieces[1:]:
        factor_of = factor_of * one(*cut)
    return factor_of


def normal_values(rng, dims, spread, limit, cuts=(), dtype=jnp.bfloat16):
    values = jax.random.normal(rng, dims, jnp.float32) * spread
    if len(cuts) > 0:
        values = level_of(rng, dims, cuts, -0.22, 0.18) * values
    return jnp.clip(values, min=-limit, max=limit).astype(dtype)


def setup_inputs(seed: int = 0, part: int = 0) -> dict:
    streams_of = jax.random.split(jax.random.key(seed), 13)
    own_keys = jax.random.split(jax.random.fold_in(streams_of[12], part), 13)
    queries = draw_queries(jax.random.fold_in(jax.random.fold_in(streams_of[12], part), 71), part)
    cached_key_store = draw_cached_key_store(jax.random.fold_in(jax.random.fold_in(streams_of[12], part), 71), part)
    cached_value_store = normal_values(own_keys[2], (REQS, KV_HEADS, L, HEAD_SIZE), 1.0, 6.0, ((0, 16),))
    decode_step_keys = normal_values(own_keys[3], (REQS, STEPS, KV_HEADS, HEAD_SIZE), 1.0, 6.0, ((0, 16),))
    decode_step_values = normal_values(own_keys[4], (REQS, STEPS, KV_HEADS, HEAD_SIZE), 1.0, 6.0, ((0, 16),))
    request_cache_length = draw_request_cache_length(jax.random.fold_in(jax.random.fold_in(streams_of[12], part), 71), part)
    output_projection_weight = normal_values(streams_of[6], (QUERY_HEADS * HEAD_SIZE, MODEL_WIDTH), (QUERY_HEADS * HEAD_SIZE) ** -0.5, 0.09375, ((0, 4),))
    adapter_down_weight = normal_values(streams_of[7], (ADAPTER_COUNT, QUERY_HEADS * HEAD_SIZE, MAXIMUM_RANK), (QUERY_HEADS * HEAD_SIZE) ** -0.5, 0.09375, ((0, 4), (1, 4)))
    adapter_up_weight = normal_values(streams_of[8], (ADAPTER_COUNT, MAXIMUM_RANK, MODEL_WIDTH), MAXIMUM_RANK ** -0.5, 0.5, ((0, 4), (2, 4)))
    adapter_store_slot = draw_adapter_store_slot(jax.random.fold_in(streams_of[12], 71), part)
    adapter_ranks = draw_adapter_ranks(jax.random.fold_in(streams_of[12], 71), part)
    request_block_adapter = draw_request_block_adapter(jax.random.fold_in(streams_of[12], 71), part)
    return dict(queries=queries, cached_key_store=cached_key_store, cached_value_store=cached_value_store, decode_step_keys=decode_step_keys, decode_step_values=decode_step_values, request_cache_length=request_cache_length, output_projection_weight=output_projection_weight, adapter_down_weight=adapter_down_weight, adapter_up_weight=adapter_up_weight, adapter_store_slot=adapter_store_slot, adapter_ranks=adapter_ranks, request_block_adapter=request_block_adapter)


adapter_alpha = 16.0

def rounded_value(values):
    return lax.optimization_barrier(values.astype(jnp.bfloat16)).astype(jnp.float32)

def reference(queries, cached_key_store, cached_value_store, decode_step_keys, decode_step_values, request_cache_length, output_projection_weight, adapter_down_weight, adapter_up_weight, adapter_store_slot, adapter_ranks, request_block_adapter):
    req_total = queries.shape[0]
    group_size = QUERY_HEADS // KV_HEADS
    inv_root = 1.0 / math.sqrt(HEAD_SIZE)
    grouped = queries.astype(jnp.float32).reshape(req_total, STEPS, KV_HEADS, group_size, HEAD_SIZE)
    cached = jnp.einsum('rskgd,rkld->rskgl', grouped, cached_key_store.astype(jnp.float32)) * inv_root
    fresh_scores = jnp.einsum('rskgd,rtkd->rskgt', grouped, decode_step_keys.astype(jnp.float32)) * inv_root
    live_mask = jnp.arange(L)[None, :] < request_cache_length[:, None]
    cached = jnp.where(live_mask[:, None, None, None, :], cached, -jnp.inf)
    causal = jnp.arange(STEPS)[None, :] <= jnp.arange(STEPS)[:, None]
    fresh_scores = jnp.where(causal[None, :, None, None, :], fresh_scores, -jnp.inf)
    highest = jnp.maximum(lax.optimization_barrier(jnp.max(cached, -1)), lax.optimization_barrier(jnp.max(fresh_scores, -1)))[..., None]
    cached_exp = jnp.exp(cached - highest)
    fresh_exp = jnp.exp(fresh_scores - highest)
    denominator = lax.optimization_barrier(jnp.sum(cached_exp, -1, keepdims=True)) + lax.optimization_barrier(jnp.sum(fresh_exp, -1, keepdims=True))
    weight_cached = rounded_value(cached_exp / denominator)
    weight_fresh = rounded_value(fresh_exp / denominator)
    mixed_out = jnp.einsum('rskgl,rkld->rskgd', weight_cached, cached_value_store.astype(jnp.float32))
    mixed_out = mixed_out + jnp.einsum('rskgt,rtkd->rskgd', weight_fresh, decode_step_values.astype(jnp.float32))
    mixed_out = rounded_value(mixed_out).reshape(req_total * STEPS, QUERY_HEADS * HEAD_SIZE)
    share = QUERY_HEADS * HEAD_SIZE // N_TP
    base = jnp.zeros((req_total * STEPS, MODEL_WIDTH), jnp.float32)
    for group_index in range(N_TP):
        piece_in = mixed_out[:, group_index * share:(group_index + 1) * share]
        rows_in = output_projection_weight[group_index * share:(group_index + 1) * share].astype(jnp.float32)
        base = base + rounded_value(jnp.dot(piece_in, rows_in, preferred_element_type=jnp.float32))
    blocks_total = request_block_adapter.shape[0]
    per_block = req_total // blocks_total
    slot_for_block = adapter_store_slot[request_block_adapter]
    rank_for_block = adapter_ranks[request_block_adapter]
    block_row_group = mixed_out.reshape(blocks_total, per_block * STEPS, QUERY_HEADS * HEAD_SIZE)
    narrow_rank_output = jnp.einsum('pci,pif->pcf', block_row_group, adapter_down_weight[slot_for_block].astype(jnp.float32))
    column_ids = jnp.arange(MAXIMUM_RANK)[None, None, :]
    scale_factor = (adapter_alpha / rank_for_block.astype(jnp.float32))[:, None, None]
    scaled_narrow_output = rounded_value(jnp.where(column_ids < rank_for_block[:, None, None], narrow_rank_output * scale_factor, 0.0))
    adapter_change = rounded_value(jnp.einsum('lmi,lig->lmg', scaled_narrow_output, adapter_up_weight[slot_for_block].astype(jnp.float32)))
    result = base + adapter_change.reshape(req_total * STEPS, MODEL_WIDTH)
    return result.reshape(req_total, STEPS, MODEL_WIDTH).astype(jnp.bfloat16)
```

```python
import functools
import math

import jax
import jax.numpy as jnp
from jax import lax
from jax.experimental import pallas as pl
from jax.experimental.pallas import tpu as pltpu
from jax.sharding import PartitionSpec as P

adapter_alpha = 16.0
lanes = 128
f32 = jnp.float32
bf16 = jnp.bfloat16


def swap(x, axis, bit):
    n = lax.axis_size(axis)
    return lax.ppermute(x, axis, [(i, i ^ bit) for i in range(n)])


def attend_kernel(me_ref, len_ref, q_ref, k_ref, v_ref, dk_ref, dv_ref, *rest, first, n_tp):
    outs = rest[:n_tp]
    reqs, steps, width = q_ref.shape
    kv_count, cache_len, head = k_ref.shape[1:]
    group = width // head // kv_count
    feats = width // n_tp
    heads_each = feats // head
    unit = min(heads_each, group)
    rows = unit * steps
    me = me_ref[0]
    scale = math.log2(math.e) / math.sqrt(head)
    new_count = steps * kv_count
    position = lax.broadcasted_iota(jnp.int32, (rows, cache_len), 1)
    new_col = lax.broadcasted_iota(jnp.int32, (rows, new_count), 1)
    row_step = lax.broadcasted_iota(jnp.int32, (rows, new_count), 0) % steps
    causal = new_col // kv_count <= row_step
    base = first + pl.program_id(0) * reqs
    new_keys, new_values = [], []
    for r in range(reqs):
        new_keys.append(jnp.concatenate([dk_ref[r, t].astype(f32) for t in range(steps)], axis=0).astype(bf16))
        new_values.append(jnp.concatenate([dv_ref[r, t].astype(f32) for t in range(steps)], axis=0).astype(bf16))
    for p in range(n_tp):
        dest = me ^ p
        for m in range(heads_each // unit):
            kv = (dest * heads_each + m * unit) // group
            results = []
            for r in range(reqs):
                pieces = []
                for g in range(unit):
                    at = pl.multiple_of(dest * feats + (m * unit + g) * head, lanes)
                    pieces.append(q_ref[r, :, pl.ds(at, head)].astype(f32))
                query = jnp.concatenate(pieces, axis=0).astype(bf16)
                contract = (((1,), (1,)), ((), ()))
                old = lax.dot_general(query, k_ref[r, kv], contract, preferred_element_type=f32)
                new = lax.dot_general(query, new_keys[r], contract, preferred_element_type=f32)
                old = jnp.where(position < len_ref[base + r], old, -jnp.inf)
                new = jnp.where(causal & (new_col % kv_count == kv), new, -jnp.inf)
                top = jnp.maximum(jnp.max(old, -1, keepdims=True), jnp.max(new, -1, keepdims=True))
                old = jnp.exp2((old - top) * scale)
                new = jnp.exp2((new - top) * scale)
                total = jnp.sum(old, -1, keepdims=True) + jnp.sum(new, -1, keepdims=True)
                mixed = jnp.dot(old.astype(bf16), v_ref[r, kv], preferred_element_type=f32)
                mixed += jnp.dot(new.astype(bf16), new_values[r], preferred_element_type=f32)
                results.append(mixed / total)
            for g in range(unit):
                stacked = jnp.concatenate([o[g * steps : (g + 1) * steps] for o in results], axis=0)
                col = (m * unit + g) * head
                outs[p][:, col : col + head] = stacked.astype(bf16)


def attend(q, keys, values, new_keys, new_values, lengths, me, first, count, n_tp):
    _, steps, width = q.shape
    kv_count, cache_len, head = keys.shape[1:]
    reqs = 4
    feats = width // n_tp
    off = first // reqs
    return pl.pallas_call(
        functools.partial(attend_kernel, first=first, n_tp=n_tp),
        grid_spec=pltpu.PrefetchScalarGridSpec(
            num_scalar_prefetch=2,
            grid=(count // reqs,),
            in_specs=[
                pl.BlockSpec((reqs, steps, width), lambda i, *_: (i + off, 0, 0)),
                pl.BlockSpec((reqs, kv_count, cache_len, head), lambda i, *_: (i + off, 0, 0, 0)),
                pl.BlockSpec((reqs, kv_count, cache_len, head), lambda i, *_: (i + off, 0, 0, 0)),
                pl.BlockSpec((reqs, steps, kv_count, head), lambda i, *_: (i + off, 0, 0, 0)),
                pl.BlockSpec((reqs, steps, kv_count, head), lambda i, *_: (i + off, 0, 0, 0)),
            ],
            out_specs=[pl.BlockSpec((reqs * steps, feats), lambda i, *_: (i, 0))] * n_tp,
        ),
        out_shape=[jax.ShapeDtypeStruct((count * steps, feats), bf16)] * n_tp,
        compiler_params=pltpu.CompilerParams(vmem_limit_bytes=48 << 20),
        cost_estimate=pl.CostEstimate(
            flops=count * steps * width * cache_len * 4,
            bytes_accessed=count * kv_count * cache_len * head * 4,
            transcendentals=count * steps * width // head * cache_len,
        ),
        name="attention",
    )(me, lengths, q, keys, values, new_keys, new_values)


def project_kernel(order_ref, home_ref, local_ref, *refs, n_tp, n_rep, per_block_of, with_low):
    pieces, refs = refs[:n_tp], refs[n_tp:]
    w_ref, refs = refs[0], refs[1:]
    downs, refs = refs[:n_rep], refs[n_rep:]
    if with_low:
        out_ref, low_ref, x_ref = refs
    else:
        out_ref, x_ref = refs
    step = pl.program_id(0)
    rows = pieces[0].shape[0]
    me = order_ref[pl.num_programs(0)]

    @pl.when(step == 0)
    def _():
        for p in range(n_tp):
            x_ref[pl.ds(pl.multiple_of((me ^ p) * rows, rows), rows), :] = pieces[p][...]

    tile = w_ref.shape[1]
    at = pl.multiple_of(step * tile, tile)
    out_ref[:, pl.ds(at, tile)] = jnp.dot(x_ref[...], w_ref[...], preferred_element_type=f32).astype(bf16)

    if with_low:
        wide = out_ref.shape[1] - lanes

        @pl.when(step == 0)
        def _():
            for t in range(n_tp):
                b = per_block_of(t)
                for i in range(n_rep):

                    @pl.when(home_ref[b] == i)
                    def _():
                        got = jnp.dot(
                            x_ref[t * rows : (t + 1) * rows, :],
                            downs[i][local_ref[b]],
                            preferred_element_type=f32,
                        )
                        low_ref[t * rows : (t + 1) * rows, :] = got
                        out_ref[t * rows : (t + 1) * rows, wide:] = got.astype(bf16)


def project(pieces, weight, downs, order, home, local, columns, per_block_of, tile):
    n_tp, n_rep = len(pieces), len(downs)
    rows, feats = pieces[0].shape
    total = rows * n_tp
    with_low = n_rep > 0
    held, rank = downs[0].shape[0::2] if with_low else (0, 0)
    out_shape = [jax.ShapeDtypeStruct((total, columns + (lanes if with_low else 0)), bf16)]
    if with_low:
        out_shape.append(jax.ShapeDtypeStruct((total, rank), f32))
    whole = lambda s: pl.BlockSpec(s.shape, lambda i, *_: (0,) * len(s.shape))
    return pl.pallas_call(
        functools.partial(
            project_kernel, n_tp=n_tp, n_rep=n_rep, per_block_of=per_block_of, with_low=with_low
        ),
        grid_spec=pltpu.PrefetchScalarGridSpec(
            num_scalar_prefetch=3,
            grid=(columns // tile,),
            in_specs=[whole(p) for p in pieces]
            + [pl.BlockSpec((feats, tile), lambda i, order, *_: (0, order[i]))]
            + [whole(d) for d in downs],
            out_specs=[whole(s) for s in out_shape],
            scratch_shapes=[pltpu.VMEM((total, feats), bf16)],
        ),
        out_shape=out_shape,
        compiler_params=pltpu.CompilerParams(vmem_limit_bytes=48 << 20),
        cost_estimate=pl.CostEstimate(
            flops=2 * total * feats * columns,
            bytes_accessed=feats * columns * 2 + total * (feats + columns) * 2,
            transcendentals=0,
        ),
        name="projection",
    )(order, home, local, *pieces, weight, *downs)


def combine_kernel(keep_ref, got_ref, got_low_ref, low_ref, send_ref, low_out_ref):
    wide = keep_ref.shape[1]
    send_ref[:, :wide] = (keep_ref[...].astype(f32) + got_ref[...].astype(f32)).astype(bf16)
    low = low_ref[...] + got_low_ref[...].astype(f32)
    low_out_ref[...] = low
    send_ref[:, wide:] = low.astype(bf16)


def combine(keep, got, low):
    rows, columns = keep.shape
    half = columns // 2
    rank = low.shape[1]
    return pl.pallas_call(
        combine_kernel,
        grid=(1,),
        in_specs=[
            pl.BlockSpec((rows, half), lambda i: (0, 0)),
            pl.BlockSpec((rows, half), lambda i: (0, 0)),
            pl.BlockSpec((rows, rank), lambda i: (0, columns // rank)),
            pl.BlockSpec((rows, rank), lambda i: (0, 0)),
        ],
        out_specs=[
            pl.BlockSpec((rows, half + rank), lambda i: (0, 0)),
            pl.BlockSpec((rows, rank), lambda i: (0, 0)),
        ],
        out_shape=[
            jax.ShapeDtypeStruct((rows, half + rank), bf16),
            jax.ShapeDtypeStruct((rows, rank), f32),
        ],
        compiler_params=pltpu.CompilerParams(vmem_limit_bytes=48 << 20),
        cost_estimate=pl.CostEstimate(
            flops=rows * half, bytes_accessed=rows * half * 6, transcendentals=0
        ),
        name="combine",
    )(keep, got, got, low)


def finish_kernel(home_ref, local_ref, rank_ref, keep_ref, got_ref, low_ref, *refs, n_rep, per_block_of):
    ups, refs = refs[:n_rep], refs[n_rep:]
    out_ref, delta_ref = refs[-2:]
    b = per_block_of(pl.program_id(0))
    rank = rank_ref[b]
    reqs, steps, columns = out_ref.shape
    low = low_ref[...] + got_ref[:, columns:].astype(f32)
    column = lax.broadcasted_iota(jnp.int32, low.shape, 1)
    scaled = jnp.where(column < rank, low * (adapter_alpha / rank.astype(f32)), 0.0).astype(bf16)
    for i in range(n_rep):

        @pl.when(home_ref[b] == i)
        def _():
            delta_ref[...] = jnp.dot(scaled, ups[i][local_ref[b]], preferred_element_type=f32)

    delta = delta_ref[...].astype(bf16).astype(f32)
    done = keep_ref[...] + got_ref[:, :columns].astype(f32) + delta
    for r in range(reqs):
        out_ref[r] = done[r * steps : (r + 1) * steps].astype(bf16)


def finish(keep, got, low, ups, home, local, ranks, held, reqs, steps, chunk, chunks, n_tp, per_block_of):
    columns = keep.shape[1]
    rows = reqs * steps
    n_rep = len(ups)
    rank = low.shape[1]
    operands = [home, local, ranks, keep, got, low, *ups]
    in_specs = [
        pl.BlockSpec((rows, columns), lambda t, *_: (t, 0)),
        pl.BlockSpec((rows, columns + rank), lambda t, *_: (t, 0)),
        pl.BlockSpec((rows, rank), lambda t, *_: (t, 0)),
    ] + [pl.BlockSpec(u.shape, lambda t, *_: (0, 0, 0)) for u in ups]
    aliases = {}
    if held is not None:
        aliases = {len(operands): 0}
        operands.append(held)
        in_specs.append(pl.BlockSpec(memory_space=pl.ANY))
    return pl.pallas_call(
        functools.partial(finish_kernel, n_rep=n_rep, per_block_of=per_block_of),
        grid_spec=pltpu.PrefetchScalarGridSpec(
            num_scalar_prefetch=3,
            grid=(n_tp,),
            in_specs=in_specs,
            out_specs=pl.BlockSpec((reqs, steps, columns), lambda t, *_: (t * chunks + chunk, 0, 0)),
            scratch_shapes=[pltpu.VMEM((rows, columns), f32)],
        ),
        out_shape=jax.ShapeDtypeStruct((n_tp * reqs * chunks, steps, columns), bf16),
        input_output_aliases=aliases,
        compiler_params=pltpu.CompilerParams(vmem_limit_bytes=48 << 20),
        cost_estimate=pl.CostEstimate(
            flops=2 * n_tp * rows * rank * columns,
            bytes_accessed=n_tp * rows * columns * 8 + n_rep * rank * columns * 4,
            transcendentals=0,
        ),
        name="finish",
    )(*operands)


def halving_order(n):
    if n == 1:
        return [0]
    rest = halving_order(n // 2)
    return [2 * u + 1 for u in rest] + [2 * u for u in rest]


def on_device(
    queries,
    cached_key_store,
    cached_value_store,
    decode_step_keys,
    decode_step_values,
    request_cache_length,
    output_projection_weight,
    adapter_down_weight,
    adapter_up_weight,
    adapter_store_slot,
    adapter_ranks,
    request_block_adapter,
):
    n_tp, n_rep = lax.axis_size("tp"), lax.axis_size("rep")
    me, my_rep = lax.axis_index("tp"), lax.axis_index("rep")
    reqs, steps, width = queries.shape
    held_adapters = adapter_down_weight.shape[0]
    blocks = request_block_adapter.shape[0]
    columns = width // n_tp
    chunks = 2 if reqs % 8 == 0 else 1
    count = reqs // chunks
    per_block = reqs * n_tp // blocks

    def per_block_of(t):
        return t * reqs // per_block

    downs, ups = {0: adapter_down_weight}, {0: adapter_up_weight}
    bit = n_rep // 2
    while bit >= 1:
        for p in list(downs):
            downs[p ^ bit] = swap(downs[p], "rep", bit)
            ups[p ^ bit] = swap(ups[p], "rep", bit)
        bit //= 2
    downs = [downs[p] for p in range(n_rep)]
    ups = [ups[p] for p in range(n_rep)]

    slot = adapter_store_slot[request_block_adapter]
    ranks = adapter_ranks[request_block_adapter]
    home = (slot // held_adapters) ^ my_rep
    local = slot % held_adapters

    me_list = me[None].astype(jnp.int32)
    tile = min(columns, 512)
    per = columns // tile
    owners = me ^ jnp.array(halving_order(n_tp), jnp.int32)
    tiles = (owners[:, None] * per + jnp.arange(per, dtype=jnp.int32)[None, :]).reshape(-1)
    half = tiles.shape[0] // 2
    first_order = jnp.concatenate([tiles[:half], me_list])
    second_order = jnp.concatenate([tiles[half:], me_list])

    pieces = []
    for c in range(chunks):
        own = attend(
            queries,
            cached_key_store,
            cached_value_store,
            decode_step_keys,
            decode_step_values,
            request_cache_length,
            me_list,
            c * count,
            count,
            n_tp,
        )
        pieces.append([own[0]] + [swap(own[p], "tp", p) for p in range(1, n_tp)])

    result = None
    for c in range(chunks):
        send, low = project(
            pieces[c], output_projection_weight, downs, first_order, home, local, width // 2, per_block_of, tile
        )
        got = swap(send, "tp", 1)
        (keep,) = project(
            pieces[c], output_projection_weight, [], second_order, home, local, width // 2, per_block_of, tile
        )
        bit = 2
        while bit < n_tp:
            wide = keep.shape[1]
            send, low = combine(keep, got, low)
            rest = keep[:, wide // 2 :].astype(f32) + got[:, wide // 2 : wide].astype(f32)
            got = swap(send, "tp", bit)
            keep = rest
            bit *= 2
        result = finish(
            keep, got, low, ups, home, local, ranks, result, count, steps, c, chunks, n_tp, per_block_of
        )
    return result


def solution(mesh):
    placed = (
        P(("parts", "rep", "tp"), None, None),
        P(("parts", "rep", "tp"), None, None, None),
        P(("parts", "rep", "tp"), None, None, None),
        P(("parts", "rep", "tp"), None, None, None),
        P(("parts", "rep", "tp"), None, None, None),
        P(("parts", "rep", "tp")),
        P("tp", None),
        P("rep", "tp", None),
        P("rep", None, "tp"),
        P(),
        P(),
        P("rep"),
    )
    return jax.shard_map(
        on_device,
        mesh=mesh,
        in_specs=placed,
        out_specs=P(("parts", "rep"), None, "tp"),
        check_vma=False,
    )
```

```python
import functools
import math

import jax
import jax.numpy as jnp
from jax import lax
from jax.experimental import pallas as pl
from jax.experimental.pallas import tpu as pltpu
from jax.sharding import PartitionSpec as P

adapter_alpha = 16.0
lanes = 128
f32 = jnp.float32
bf16 = jnp.bfloat16
hint = pl.CostEstimate(flops=1, bytes_accessed=1, transcendentals=0)


def swap(x, axis, bit):
    n = lax.axis_size(axis)
    return lax.ppermute(x, axis, [(i, i ^ bit) for i in range(n)])


def in_hbm(x):
    return pltpu.with_memory_space_constraint(x, pltpu.HBM)


def in_vmem(x):
    return pltpu.with_memory_space_constraint(x, pltpu.VMEM)


def attend_kernel(me_ref, len_ref, q_ref, dk_ref, dv_ref, *refs, pieces, n_tp, kv_count):
    count = len(pieces)
    k_refs, v_refs, outs = refs[:count], refs[count : 2 * count], refs[-count:]
    reqs, steps, width = q_ref.shape
    cache_len, head = k_refs[0].shape[2:]
    heads_each = width // head // n_tp
    group = width // head // kv_count
    feats = heads_each * head
    rows = heads_each * steps
    me = me_ref[0]
    scale = math.log2(math.e) / math.sqrt(head)
    fresh = steps * kv_count
    shape = (count * rows, lanes)
    row = lax.broadcasted_iota(jnp.int32, shape, 0)
    col = lax.broadcasted_iota(jnp.int32, shape, 1)
    row_kv = jnp.zeros(shape, jnp.int32)
    for u, p in enumerate(pieces):
        row_kv = jnp.where(row // rows == u, (me ^ p) * heads_each // group, row_kv)
    visible = (col % kv_count == row_kv) & (col // kv_count <= row % steps) & (col < fresh)
    base = pl.program_id(0) * reqs
    contract = (((1,), (1,)), ((), ()))
    pad = jnp.zeros((lanes - fresh, head), f32)

    def steps_of(ref, r):
        return jnp.concatenate([ref[r, t].astype(f32) for t in range(steps)] + [pad], axis=0).astype(bf16)

    old, new = [], []
    for r in range(reqs):
        parts = []
        for p in pieces:
            for g in range(heads_each):
                at = pl.multiple_of((me ^ p) * feats + g * head, lanes)
                parts.append(q_ref[r, :, pl.ds(at, head)].astype(f32))
        query = jnp.concatenate(parts, axis=0).astype(bf16)
        old.append(
            jnp.concatenate(
                [
                    lax.dot_general(
                        query[u * rows : (u + 1) * rows], k_refs[u][r, 0], contract, preferred_element_type=f32
                    )
                    for u in range(count)
                ],
                axis=0,
            )
        )
        new.append(lax.dot_general(query, steps_of(dk_ref, r), contract, preferred_element_type=f32))
    share, old_weight, new_weight = [], [], []
    for r in range(reqs):
        a = jnp.where(col < len_ref[base + r], old[r], -jnp.inf)
        b = jnp.where(visible, new[r], -jnp.inf)
        top = jnp.max(jnp.maximum(a, b), -1, keepdims=True)
        a = jnp.exp2((a - top) * scale)
        b = jnp.exp2((b - top) * scale)
        share.append(1.0 / jnp.sum(a + b, -1, keepdims=True))
        old_weight.append(a.astype(bf16))
        new_weight.append(b.astype(bf16))
    mixed = []
    for r in range(reqs):
        o = jnp.concatenate(
            [
                jnp.dot(old_weight[r][u * rows : (u + 1) * rows], v_refs[u][r, 0], preferred_element_type=f32)
                for u in range(count)
            ],
            axis=0,
        )
        o += jnp.dot(new_weight[r], steps_of(dv_ref, r), preferred_element_type=f32)
        mixed.append(o * share[r])
    for u in range(count):
        for g in range(heads_each):
            at = u * rows + g * steps
            stacked = jnp.concatenate([o[at : at + steps] for o in mixed], axis=0)
            outs[u][:, g * head : (g + 1) * head] = stacked.astype(bf16)


def attend(q, keys, values, new_keys, new_values, lengths, me, pieces, n_tp, waits=()):
    count, steps, width = q.shape
    kv_count, cache_len, head = keys.shape[1:]
    heads_each = width // head // n_tp
    group = width // head // kv_count
    assert group % heads_each == 0
    reqs = min(count, 8)
    feats = width // n_tp

    def cache_spec(p):
        return pl.BlockSpec(
            (reqs, 1, cache_len, head), lambda i, me, *_: (i, (me[0] ^ p) * heads_each // group, 0, 0)
        )

    q, keys, values, new_keys, new_values, lengths = map(
        in_hbm, (q, keys, values, new_keys, new_values, lengths)
    )
    return pl.pallas_call(
        functools.partial(attend_kernel, pieces=pieces, n_tp=n_tp, kv_count=kv_count),
        grid_spec=pltpu.PrefetchScalarGridSpec(
            num_scalar_prefetch=2,
            grid=(count // reqs,),
            in_specs=[
                pl.BlockSpec((reqs, steps, width), lambda i, *_: (i, 0, 0)),
                pl.BlockSpec((reqs, steps, kv_count, head), lambda i, *_: (i, 0, 0, 0)),
                pl.BlockSpec((reqs, steps, kv_count, head), lambda i, *_: (i, 0, 0, 0)),
            ]
            + [cache_spec(p) for p in pieces] * 2
            + [pl.BlockSpec(memory_space=pl.ANY)] * len(waits),
            out_specs=[pl.BlockSpec((reqs * steps, feats), lambda i, *_: (i, 0))] * len(pieces),
        ),
        out_shape=[jax.ShapeDtypeStruct((count * steps, feats), bf16)] * len(pieces),
        compiler_params=pltpu.CompilerParams(vmem_limit_bytes=32 << 20),
        cost_estimate=hint,
        name="attention",
    )(me, lengths, q, new_keys, new_values, *([keys] * len(pieces)), *([values] * len(pieces)), *waits)


def weight_copies(me, w_ref, out, sems, owners, columns, start, width):
    copies = []
    for u, p in enumerate(owners):
        at = pl.multiple_of((me ^ p) * columns + start, lanes)
        copies.append(
            pltpu.make_async_copy(
                w_ref.at[:, pl.ds(at, width)], out.at[:, u * width : (u + 1) * width], sems.at[u]
            )
        )
    return copies


def load_kernel(me_ref, w_ref, *refs, owners, part, columns):
    out_ref, sems = refs[-2:]
    copies = weight_copies(me_ref[0], w_ref, out_ref, sems, owners, columns, 0, part)
    for copy in copies:
        copy.start()
    for copy in copies:
        copy.wait()


def load(weight, me, owners, part, columns, waits):
    return pl.pallas_call(
        functools.partial(load_kernel, owners=owners, part=part, columns=columns),
        in_specs=[pl.BlockSpec(memory_space=pltpu.SMEM)]
        + [pl.BlockSpec(memory_space=pl.ANY)] * (1 + len(waits)),
        out_specs=pl.BlockSpec(memory_space=pltpu.VMEM),
        out_shape=pltpu.VMEM((weight.shape[0], len(owners) * part), weight.dtype),
        scratch_shapes=[pltpu.SemaphoreType.DMA((len(owners),))],
        compiler_params=pltpu.CompilerParams(vmem_limit_bytes=8 << 20),
        cost_estimate=hint,
        name="load",
    )(me, in_hbm(weight), *waits)


def block_place(table, b):
    rep_ref, adapter_ref, slot_ref, rank_ref, held = table
    adapter = adapter_ref[b]
    slot = slot_ref[adapter]
    return (slot // held) ^ rep_ref[0], slot % held, rank_ref[adapter]


def project_kernel(me_ref, *refs):
    *pieces, w_ref, out_ref, x_ref = refs
    rows = pieces[0].shape[0]
    for p, piece in enumerate(pieces):
        x_ref[pl.ds(pl.multiple_of((me_ref[0] ^ p) * rows, rows), rows), :] = piece[...]
    out_ref[...] = jnp.dot(x_ref[...], w_ref[...], preferred_element_type=f32).astype(bf16)


def project(pieces, weight, me):
    total = sum(x.shape[0] for x in pieces)
    return pl.pallas_call(
        project_kernel,
        in_specs=[pl.BlockSpec(memory_space=pltpu.SMEM)]
        + [pl.BlockSpec(memory_space=pltpu.VMEM)] * (len(pieces) + 1),
        out_specs=[pl.BlockSpec(memory_space=pltpu.VMEM)] * 2,
        out_shape=[
            jax.ShapeDtypeStruct((total, weight.shape[1]), bf16),
            jax.ShapeDtypeStruct((total, pieces[0].shape[1]), bf16),
        ],
        compiler_params=pltpu.CompilerParams(vmem_limit_bytes=8 << 20),
        cost_estimate=hint,
        name="projection",
    )(me, *pieces, in_vmem(weight))


def project_rest_kernel(me_ref, *refs, order, widths, columns, adapters, per_block, held):
    table, refs = (*refs[:4], held), refs[4:]
    x_ref, w_ref, downs, refs = refs[0], refs[1], refs[2 : 2 + adapters], refs[2 + adapters :]
    parts, owners = len(widths), len(order) // 2
    outs, keep_ref, low_ref = refs[: parts - 1], refs[parts - 1], refs[parts]
    nears, sems = refs[parts + 1 : -1], refs[-1]
    starts = [sum(widths[:q]) for q in range(parts)]
    jobs = [(order[:owners], q) for q in range(1, parts)] + [(order[owners:], q) for q in range(parts)]
    copies = [
        weight_copies(me_ref[0], w_ref, near, sems.at[h], relative, columns, starts[q], widths[q])
        for h, (near, (relative, q)) in enumerate(zip(nears, jobs))
    ]
    for group in copies:
        for copy in group:
            copy.start()
    for start in range(0, x_ref.shape[0], per_block):
        home, place, _ = block_place(table, start // per_block)
        here = slice(start, start + per_block)
        for i in range(adapters):

            @pl.when(home == i)
            def _():
                got = jnp.dot(x_ref[here, :], downs[i][place], preferred_element_type=f32)
                low_ref[here, :] = got
                outs[0][here, owners * widths[1] :] = got.astype(bf16)

    for h, (near, (_, q)) in enumerate(zip(nears, jobs)):
        for copy in copies[h]:
            copy.wait()
        got = jnp.dot(x_ref[...], near[...], preferred_element_type=f32).astype(bf16)
        wide = owners * widths[q]
        if h < parts - 1:
            outs[h][:, :wide] = got
        else:
            keep_ref[:, owners * starts[q] : owners * starts[q] + wide] = got


def project_rest(x, weight, downs, me, table, order, widths, columns, per_block):
    rows, feats = x.shape
    parts, owners = len(widths), len(order) // 2
    held, _, rank = downs[0].shape
    shapes = [(rows, owners * w) for w in (*widths[1:], columns)]
    shapes[0] = (rows, owners * widths[1] + rank)
    vmem = pl.BlockSpec(memory_space=pltpu.VMEM)
    return pl.pallas_call(
        functools.partial(
            project_rest_kernel,
            order=order,
            widths=widths,
            columns=columns,
            adapters=len(downs),
            per_block=per_block,
            held=held,
        ),
        in_specs=[pl.BlockSpec(memory_space=pltpu.SMEM)] * (1 + len(table))
        + [vmem, pl.BlockSpec(memory_space=pl.ANY)]
        + [vmem] * len(downs),
        out_specs=[vmem] * (parts + 1),
        out_shape=[jax.ShapeDtypeStruct(shape, bf16) for shape in shapes]
        + [jax.ShapeDtypeStruct((rows, rank), f32)],
        scratch_shapes=[pltpu.VMEM((feats, owners * w), weight.dtype) for w in (*widths[1:], *widths)]
        + [pltpu.SemaphoreType.DMA((2 * parts - 1, owners))],
        compiler_params=pltpu.CompilerParams(vmem_limit_bytes=20 << 20),
        cost_estimate=hint,
        name="projection_rest",
    )(me, *map(in_hbm, table), x, in_hbm(weight), *downs)


def combine_kernel(*refs, offsets, wide, with_low, waits):
    refs = refs[waits:]
    n = len(offsets)
    addends, refs = refs[:n], refs[n:]
    total = sum(a[:, off : off + wide].astype(f32) for a, off in zip(addends, offsets))
    if with_low:
        low_ref, send_ref, low_out_ref = refs
        low = low_ref[...] + addends[-1][:, addends[-1].shape[1] - lanes :].astype(f32)
        low_out_ref[...] = low
        send_ref[:, wide:] = low.astype(bf16)
    else:
        (send_ref,) = refs
    send_ref[:, :wide] = total.astype(bf16)


def combine(addends, wide, low, waits):
    arrays = [a for a, _ in addends]
    rows = arrays[0].shape[0]
    rank = 0 if low is None else low.shape[1]
    out_shape = [jax.ShapeDtypeStruct((rows, wide + rank), bf16)]
    if low is not None:
        arrays.append(low)
        out_shape.append(jax.ShapeDtypeStruct((rows, rank), f32))
    return pl.pallas_call(
        functools.partial(
            combine_kernel,
            offsets=[off for _, off in addends],
            wide=wide,
            with_low=low is not None,
            waits=len(waits),
        ),
        in_specs=[pl.BlockSpec(memory_space=pl.ANY)] * len(waits)
        + [pl.BlockSpec(memory_space=pltpu.VMEM)] * len(arrays),
        out_specs=[pl.BlockSpec(memory_space=pltpu.VMEM)] * len(out_shape),
        out_shape=out_shape,
        compiler_params=pltpu.CompilerParams(vmem_limit_bytes=8 << 20),
        cost_estimate=hint,
        name="combine",
    )(*waits, *arrays)


def finish_kernel(*refs, offsets, widths, first, n_rep, per_block, held):
    table, refs = (*refs[:4], held), refs[4:]
    addends = []
    for part_offsets in offsets:
        addends.append(list(zip(refs, part_offsets)))
        refs = refs[len(part_offsets) :]
    low_ref, got_ref, refs = refs[0], refs[1], refs[2:]
    ups, refs = refs[:n_rep], refs[n_rep:]
    out_ref, delta_ref, done_ref, sem = refs[-4:]
    steps = out_ref.shape[1]
    total_rows, rank_most = low_ref.shape
    low = low_ref[...] + got_ref[:, got_ref.shape[1] - rank_most :].astype(f32)
    column = lax.broadcasted_iota(jnp.int32, (per_block, rank_most), 1)
    here_columns = slice(first, first + sum(widths))
    for start in range(0, total_rows, per_block):
        home, place, rank = block_place(table, start // per_block)
        here = slice(start, start + per_block)
        factor = adapter_alpha / rank.astype(f32)
        scaled = jnp.where(column < rank, low[here] * factor, 0.0).astype(bf16)
        for i in range(n_rep):

            @pl.when(home == i)
            def _():
                delta_ref[here, :] = jnp.dot(
                    scaled, ups[i][place, :, here_columns], preferred_element_type=f32
                )

    for start in range(0, total_rows, per_block):
        here = slice(start, start + per_block)
        at = 0
        for pairs, width in zip(addends, widths):
            there = slice(at, at + width)
            total = sum(a[here, off : off + width].astype(f32) for a, off in pairs)
            total += delta_ref[here, there].astype(bf16).astype(f32)
            for r in range(per_block // steps):
                done_ref[start // steps + r, :, there] = total[r * steps : (r + 1) * steps].astype(bf16)
            at += width
    copy = pltpu.make_async_copy(done_ref, out_ref.at[:, :, here_columns], sem)
    copy.start()
    copy.wait()


def finish(finals, widths, first, low, got, ups, table, held_out, steps, columns, per_block):
    total, rank = low.shape
    wide = sum(widths)
    operands = [a for addends in finals for a, _ in addends] + [low, got, *ups]
    in_specs = [pl.BlockSpec(memory_space=pltpu.SMEM)] * len(table)
    in_specs += [pl.BlockSpec(memory_space=pltpu.VMEM)] * len(operands)
    aliases = {}
    if held_out is not None:
        aliases = {len(table) + len(operands): 0}
        operands.append(held_out)
        in_specs.append(pl.BlockSpec(memory_space=pl.ANY))
    return pl.pallas_call(
        functools.partial(
            finish_kernel,
            offsets=[[off for _, off in addends] for addends in finals],
            widths=widths,
            first=first,
            n_rep=len(ups),
            per_block=per_block,
            held=ups[0].shape[0],
        ),
        in_specs=in_specs,
        out_specs=pl.BlockSpec(memory_space=pl.ANY),
        out_shape=jax.ShapeDtypeStruct((total // steps, steps, columns), bf16),
        scratch_shapes=[
            pltpu.VMEM((total, wide), f32),
            pltpu.VMEM((total // steps, steps, wide), bf16),
            pltpu.SemaphoreType.DMA,
        ],
        input_output_aliases=aliases,
        compiler_params=pltpu.CompilerParams(vmem_limit_bytes=12 << 20),
        cost_estimate=hint,
        name="finish",
    )(*map(in_hbm, table), *operands)


def halving_order(n):
    if n == 1:
        return [0]
    rest = halving_order(n // 2)
    return [2 * u + 1 for u in rest] + [2 * u for u in rest]


def after(x, *others):
    return lax.optimization_barrier((x, *others))[0]


def on_device(
    queries,
    cached_key_store,
    cached_value_store,
    decode_step_keys,
    decode_step_values,
    request_cache_length,
    output_projection_weight,
    adapter_down_weight,
    adapter_up_weight,
    adapter_store_slot,
    adapter_ranks,
    request_block_adapter,
):
    n_tp, n_rep = lax.axis_size("tp"), lax.axis_size("rep")
    me = lax.axis_index("tp")[None].astype(jnp.int32)
    my_rep = lax.axis_index("rep")[None].astype(jnp.int32)
    reqs, steps, width = queries.shape
    blocks = request_block_adapter.shape[0]
    columns = width // n_tp
    per_block = reqs * n_tp * steps // blocks
    table = (my_rep, request_block_adapter, adapter_store_slot, adapter_ranks)

    arrays = (
        queries,
        cached_key_store,
        cached_value_store,
        decode_step_keys,
        decode_step_values,
        request_cache_length,
    )
    order = halving_order(n_tp)
    eighth = columns // 8
    widths = [4 * eighth, 3 * eighth, 1 * eighth] if eighth % lanes == 0 else [columns // 2] * 2
    parts = len(widths)
    starts = [sum(widths[:q]) for q in range(parts)]
    owners = n_tp // 2
    top_bit = n_rep // 2

    def relay(x, across, go):
        held = {0: after(x, go), top_bit: after(across, go)}
        bit = top_bit // 2
        while bit >= 1:
            for p in list(held):
                held[p ^ bit] = swap(held[p], "rep", bit)
            bit //= 2
        return [held[p] for p in range(n_rep)]

    down_across = swap(adapter_down_weight, "rep", top_bit)
    far, near = range(1, n_tp), range(1)
    own = dict(zip(far, attend(*arrays, me, far, n_tp)))
    pieces = {p: swap(own[p], "tp", p) for p in reversed(far)}
    own.update(zip(near, attend(*arrays, me, near, n_tp, [own[n_tp - 1]])))
    pieces[0] = own[0]
    weight = load(output_projection_weight, me, order[:owners], widths[0], columns, [own[0]])

    send, x = project([pieces[p] for p in range(n_tp)], weight, me)
    downs = relay(adapter_down_weight, down_across, send)
    up_across = swap(after(adapter_up_weight, send), "rep", top_bit)
    *sends, keep, low = project_rest(
        x, output_projection_weight, downs, me, table, order, widths, columns, per_block
    )
    gots = [swap(send, "tp", 1) for send in (send, *sends)]
    finals, last = [], [keep]
    for q in range(parts):
        addends = [(keep, owners * starts[q]), (gots[q], 0)]
        wide = owners * widths[q]
        bit = 2
        while bit < n_tp:
            wide //= 2
            out = combine(addends, wide, low if q == 1 else None, last)
            if q == 1:
                low = out[1]
            got = swap(out[0], "tp", bit)
            if bit == 2:
                last = [out[0]]
            addends = [(a, off + wide) for a, off in addends] + [(got, 0)]
            bit *= 2
        finals.append(addends)
        if q == 0:
            ups = relay(adapter_up_weight, up_across, last[0])
        if q == 1:
            low_parts = (low, got)

    result = None
    for group in (slice(0, parts - 1), slice(parts - 1, parts)):
        result = finish(
            finals[group],
            widths[group],
            starts[group.start],
            *low_parts,
            ups,
            table,
            result,
            steps,
            columns,
            per_block,
        )
    return result


def solution(mesh):
    placed = (
        P(("parts", "rep", "tp"), None, None),
        P(("parts", "rep", "tp"), None, None, None),
        P(("parts", "rep", "tp"), None, None, None),
        P(("parts", "rep", "tp"), None, None, None),
        P(("parts", "rep", "tp"), None, None, None),
        P(("parts", "rep", "tp")),
        P("tp", None),
        P("rep", "tp", None),
        P("rep", None, "tp"),
        P(),
        P(),
        P("rep"),
    )
    return jax.shard_map(
        on_device,
        mesh=mesh,
        in_specs=placed,
        out_specs=P(("parts", "rep"), None, "tp"),
        check_vma=False,
    )
```

```python
import functools
import math

import jax
import jax.numpy as jnp
from jax import lax
from jax.experimental import pallas as pl
from jax.experimental.pallas import tpu as pltpu
from jax.sharding import PartitionSpec as P

adapter_alpha = 16.0
lanes = 128
f32 = jnp.float32
bf16 = jnp.bfloat16
hint = pl.CostEstimate(flops=1, bytes_accessed=1, transcendentals=0)
long = pl.CostEstimate(flops=10**11, bytes_accessed=10**9, transcendentals=0)


def swap(x, axis, bit):
    n = lax.axis_size(axis)
    return lax.ppermute(x, axis, [(i, i ^ bit) for i in range(n)])


def in_hbm(x):
    return pltpu.with_memory_space_constraint(x, pltpu.HBM)


def in_vmem(x):
    return pltpu.with_memory_space_constraint(x, pltpu.VMEM)


def attend_kernel(me_ref, len_ref, q_ref, dk_ref, dv_ref, *refs, pieces, n_tp, kv_count):
    count = len(pieces)
    k_refs, v_refs, outs = refs[:count], refs[count : 2 * count], refs[-count:]
    reqs, steps, width = q_ref.shape
    cache_len, head = k_refs[0].shape[2:]
    heads_each = width // head // n_tp
    group = width // head // kv_count
    feats = heads_each * head
    rows = heads_each * steps
    me = me_ref[0]
    scale = math.log2(math.e) / math.sqrt(head)
    fresh = steps * kv_count
    shape = (count * rows, lanes)
    row = lax.broadcasted_iota(jnp.int32, shape, 0)
    col = lax.broadcasted_iota(jnp.int32, shape, 1)
    row_kv = jnp.zeros(shape, jnp.int32)
    for u, p in enumerate(pieces):
        row_kv = jnp.where(row // rows == u, (me ^ p) * heads_each // group, row_kv)
    visible = (col % kv_count == row_kv) & (col // kv_count <= row % steps) & (col < fresh)
    base = pl.program_id(0) * reqs
    contract = (((1,), (1,)), ((), ()))
    pad = jnp.zeros((lanes - fresh, head), f32)

    def steps_of(ref, r):
        return jnp.concatenate([ref[r, t].astype(f32) for t in range(steps)] + [pad], axis=0).astype(bf16)

    old, new = [], []
    for r in range(reqs):
        parts = []
        for p in pieces:
            for g in range(heads_each):
                at = pl.multiple_of((me ^ p) * feats + g * head, lanes)
                parts.append(q_ref[r, :, pl.ds(at, head)].astype(f32))
        query = jnp.concatenate(parts, axis=0).astype(bf16)
        old.append(
            jnp.concatenate(
                [
                    lax.dot_general(
                        query[u * rows : (u + 1) * rows], k_refs[u][r, 0], contract, preferred_element_type=f32
                    )
                    for u in range(count)
                ],
                axis=0,
            )
        )
        new.append(lax.dot_general(query, steps_of(dk_ref, r), contract, preferred_element_type=f32))
    share, old_weight, new_weight = [], [], []
    for r in range(reqs):
        a = jnp.where(col < len_ref[base + r], old[r], -jnp.inf)
        b = jnp.where(visible, new[r], -jnp.inf)
        top = jnp.max(jnp.maximum(a, b), -1, keepdims=True)
        a = jnp.exp2((a - top) * scale)
        b = jnp.exp2((b - top) * scale)
        share.append(1.0 / jnp.sum(a + b, -1, keepdims=True))
        old_weight.append(a.astype(bf16))
        new_weight.append(b.astype(bf16))
    mixed = []
    for r in range(reqs):
        o = jnp.concatenate(
            [
                jnp.dot(old_weight[r][u * rows : (u + 1) * rows], v_refs[u][r, 0], preferred_element_type=f32)
                for u in range(count)
            ],
            axis=0,
        )
        o += jnp.dot(new_weight[r], steps_of(dv_ref, r), preferred_element_type=f32)
        mixed.append(o * share[r])
    for u in range(count):
        for g in range(heads_each):
            at = u * rows + g * steps
            stacked = jnp.concatenate([o[at : at + steps] for o in mixed], axis=0)
            outs[u][:, g * head : (g + 1) * head] = stacked.astype(bf16)


def attend(q, keys, values, new_keys, new_values, lengths, me, pieces, n_tp, waits=()):
    count, steps, width = q.shape
    kv_count, cache_len, head = keys.shape[1:]
    heads_each = width // head // n_tp
    group = width // head // kv_count
    assert group % heads_each == 0
    reqs = min(count, 8)
    feats = width // n_tp

    def cache_spec(p):
        return pl.BlockSpec(
            (reqs, 1, cache_len, head), lambda i, me, *_: (i, (me[0] ^ p) * heads_each // group, 0, 0)
        )

    q, keys, values, new_keys, new_values, lengths = map(
        in_hbm, (q, keys, values, new_keys, new_values, lengths)
    )
    return pl.pallas_call(
        functools.partial(attend_kernel, pieces=pieces, n_tp=n_tp, kv_count=kv_count),
        grid_spec=pltpu.PrefetchScalarGridSpec(
            num_scalar_prefetch=2,
            grid=(count // reqs,),
            in_specs=[
                pl.BlockSpec((reqs, steps, width), lambda i, *_: (i, 0, 0)),
                pl.BlockSpec((reqs, steps, kv_count, head), lambda i, *_: (i, 0, 0, 0)),
                pl.BlockSpec((reqs, steps, kv_count, head), lambda i, *_: (i, 0, 0, 0)),
            ]
            + [cache_spec(p) for p in pieces] * 2
            + [pl.BlockSpec(memory_space=pl.ANY)] * len(waits),
            out_specs=[pl.BlockSpec((reqs * steps, feats), lambda i, *_: (i, 0))] * len(pieces),
        ),
        out_shape=[jax.ShapeDtypeStruct((count * steps, feats), bf16)] * len(pieces),
        compiler_params=pltpu.CompilerParams(vmem_limit_bytes=32 << 20),
        cost_estimate=hint,
        name="attention",
    )(me, lengths, q, new_keys, new_values, *([keys] * len(pieces)), *([values] * len(pieces)), *waits)


def weight_copies(me, w_ref, out, sems, owners, columns, start, width):
    copies = []
    for u, p in enumerate(owners):
        at = pl.multiple_of((me ^ p) * columns + start, lanes)
        copies.append(
            pltpu.make_async_copy(
                w_ref.at[:, pl.ds(at, width)], out.at[:, u * width : (u + 1) * width], sems.at[u]
            )
        )
    return copies


def load_kernel(me_ref, w_ref, *refs, owners, part, columns):
    out_ref, sems = refs[-2:]
    copies = weight_copies(me_ref[0], w_ref, out_ref, sems, owners, columns, 0, part)
    for copy in copies:
        copy.start()
    for copy in copies:
        copy.wait()


def load(weight, me, owners, part, columns, waits):
    return pl.pallas_call(
        functools.partial(load_kernel, owners=owners, part=part, columns=columns),
        in_specs=[pl.BlockSpec(memory_space=pltpu.SMEM)]
        + [pl.BlockSpec(memory_space=pl.ANY)] * (1 + len(waits)),
        out_specs=pl.BlockSpec(memory_space=pltpu.VMEM),
        out_shape=pltpu.VMEM((weight.shape[0], len(owners) * part), weight.dtype),
        scratch_shapes=[pltpu.SemaphoreType.DMA((len(owners),))],
        compiler_params=pltpu.CompilerParams(vmem_limit_bytes=8 << 20),
        cost_estimate=hint,
        name="load",
    )(me, in_hbm(weight), *waits)


def block_place(table, b):
    rep_ref, adapter_ref, slot_ref, rank_ref, held = table
    adapter = adapter_ref[b]
    slot = slot_ref[adapter]
    return (slot // held) ^ rep_ref[0], slot % held, rank_ref[adapter]


def project_kernel(me_ref, *refs):
    *pieces, w_ref, out_ref, x_ref = refs
    rows = pieces[0].shape[0]
    for p, piece in enumerate(pieces):
        x_ref[pl.ds(pl.multiple_of((me_ref[0] ^ p) * rows, rows), rows), :] = piece[...]
    out_ref[...] = jnp.dot(x_ref[...], w_ref[...], preferred_element_type=f32).astype(bf16)


def project(pieces, weight, me):
    total = sum(x.shape[0] for x in pieces)
    return pl.pallas_call(
        project_kernel,
        in_specs=[pl.BlockSpec(memory_space=pltpu.SMEM)]
        + [pl.BlockSpec(memory_space=pltpu.VMEM)] * (len(pieces) + 1),
        out_specs=[pl.BlockSpec(memory_space=pltpu.VMEM)] * 2,
        out_shape=[
            jax.ShapeDtypeStruct((total, weight.shape[1]), bf16),
            jax.ShapeDtypeStruct((total, pieces[0].shape[1]), bf16),
        ],
        compiler_params=pltpu.CompilerParams(vmem_limit_bytes=8 << 20),
        cost_estimate=long,
        name="projection",
    )(me, *pieces, in_vmem(weight))


def project_rest_kernel(me_ref, x_ref, w_ref, *refs, order, widths, columns):
    parts, owners = len(widths), len(order) // 2
    outs, keep_ref = refs[: parts - 2], refs[parts - 2]
    nears, sems = refs[parts - 1 : -1], refs[-1]
    starts = [sum(widths[:q]) for q in range(parts)]
    jobs = [(order[:owners], q) for q in range(1, parts - 1)] + [(order[owners:], q) for q in range(parts)]
    copies = [
        weight_copies(me_ref[0], w_ref, near, sems.at[h], relative, columns, starts[q], widths[q])
        for h, (near, (relative, q)) in enumerate(zip(nears, jobs))
    ]
    for group in copies:
        for copy in group:
            copy.start()
    for h, (near, (_, q)) in enumerate(zip(nears, jobs)):
        for copy in copies[h]:
            copy.wait()
        got = jnp.dot(x_ref[...], near[...], preferred_element_type=f32).astype(bf16)
        if h < parts - 2:
            outs[h][...] = got
        else:
            keep_ref[:, owners * starts[q] : owners * (starts[q] + widths[q])] = got


def project_rest(x, weight, me, order, widths, columns):
    rows, feats = x.shape
    parts, owners = len(widths), len(order) // 2
    vmem = pl.BlockSpec(memory_space=pltpu.VMEM)
    return pl.pallas_call(
        functools.partial(project_rest_kernel, order=order, widths=widths, columns=columns),
        in_specs=[pl.BlockSpec(memory_space=pltpu.SMEM), vmem, pl.BlockSpec(memory_space=pl.ANY)],
        out_specs=[vmem] * (parts - 1),
        out_shape=[jax.ShapeDtypeStruct((rows, owners * w), bf16) for w in (*widths[1:-1], columns)],
        scratch_shapes=[pltpu.VMEM((feats, owners * w), weight.dtype) for w in (*widths[1:-1], *widths)]
        + [pltpu.SemaphoreType.DMA((2 * parts - 2, owners))],
        compiler_params=pltpu.CompilerParams(vmem_limit_bytes=20 << 20),
        cost_estimate=hint,
        name="projection_rest",
    )(me, x, in_hbm(weight))


def project_last_kernel(me_ref, *refs, owners, width, columns, adapters, per_block, held, waits):
    table, refs = (*refs[:4], held), refs[4:]
    x_ref, w_ref, downs = refs[0], refs[1], refs[2 : 2 + adapters]
    out_ref, low_ref, near, sems = refs[2 + adapters + waits :]
    copies = weight_copies(me_ref[0], w_ref, near, sems, owners, columns, columns - width, width)
    for copy in copies:
        copy.start()
    wide = len(owners) * width
    for start in range(0, x_ref.shape[0], per_block):
        home, place, _ = block_place(table, start // per_block)
        here = slice(start, start + per_block)
        for i in range(adapters):

            @pl.when(home == i)
            def _():
                got = jnp.dot(x_ref[here, :], downs[i][place], preferred_element_type=f32)
                low_ref[here, :] = got
                out_ref[here, wide:] = got.astype(bf16)

    for copy in copies:
        copy.wait()
    out_ref[:, :wide] = jnp.dot(x_ref[...], near[...], preferred_element_type=f32).astype(bf16)


def project_last(x, weight, downs, me, table, owners, width, columns, per_block, waits):
    rows, feats = x.shape
    held, _, rank = downs[0].shape
    wide = len(owners) * width
    vmem = pl.BlockSpec(memory_space=pltpu.VMEM)
    return pl.pallas_call(
        functools.partial(
            project_last_kernel,
            owners=owners,
            width=width,
            columns=columns,
            adapters=len(downs),
            per_block=per_block,
            held=held,
            waits=len(waits),
        ),
        in_specs=[pl.BlockSpec(memory_space=pltpu.SMEM)] * (1 + len(table))
        + [vmem, pl.BlockSpec(memory_space=pl.ANY)]
        + [vmem] * len(downs)
        + [pl.BlockSpec(memory_space=pl.ANY)] * len(waits),
        out_specs=[vmem] * 2,
        out_shape=[
            jax.ShapeDtypeStruct((rows, wide + rank), bf16),
            jax.ShapeDtypeStruct((rows, rank), f32),
        ],
        scratch_shapes=[
            pltpu.VMEM((feats, wide), weight.dtype),
            pltpu.SemaphoreType.DMA((len(owners),)),
        ],
        compiler_params=pltpu.CompilerParams(vmem_limit_bytes=16 << 20),
        cost_estimate=hint,
        name="projection_last",
    )(me, *map(in_hbm, table), x, in_hbm(weight), *downs, *waits)


def combine_kernel(*refs, offsets, wide, with_low, waits):
    refs = refs[waits:]
    n = len(offsets)
    addends, refs = refs[:n], refs[n:]
    total = sum(a[:, off : off + wide].astype(f32) for a, off in zip(addends, offsets))
    if with_low:
        low_ref, send_ref, low_out_ref = refs
        low = low_ref[...] + addends[-1][:, addends[-1].shape[1] - lanes :].astype(f32)
        low_out_ref[...] = low
        send_ref[:, wide:] = low.astype(bf16)
    else:
        (send_ref,) = refs
    send_ref[:, :wide] = total.astype(bf16)


def combine(addends, wide, low, waits):
    arrays = [a for a, _ in addends]
    rows = arrays[0].shape[0]
    rank = 0 if low is None else low.shape[1]
    out_shape = [jax.ShapeDtypeStruct((rows, wide + rank), bf16)]
    if low is not None:
        arrays.append(low)
        out_shape.append(jax.ShapeDtypeStruct((rows, rank), f32))
    return pl.pallas_call(
        functools.partial(
            combine_kernel,
            offsets=[off for _, off in addends],
            wide=wide,
            with_low=low is not None,
            waits=len(waits),
        ),
        in_specs=[pl.BlockSpec(memory_space=pl.ANY)] * len(waits)
        + [pl.BlockSpec(memory_space=pltpu.VMEM)] * len(arrays),
        out_specs=[pl.BlockSpec(memory_space=pltpu.VMEM)] * len(out_shape),
        out_shape=out_shape,
        compiler_params=pltpu.CompilerParams(vmem_limit_bytes=8 << 20),
        cost_estimate=long,
        name="combine",
    )(*waits, *arrays)


def finish_kernel(*refs, offsets, widths, first, n_rep, per_block, held):
    table, refs = (*refs[:4], held), refs[4:]
    addends = []
    for part_offsets in offsets:
        addends.append(list(zip(refs, part_offsets)))
        refs = refs[len(part_offsets) :]
    low_ref, got_ref, refs = refs[0], refs[1], refs[2:]
    ups, refs = refs[:n_rep], refs[n_rep:]
    out_ref, delta_ref, done_ref, sem = refs[-4:]
    steps = out_ref.shape[1]
    total_rows, rank_most = low_ref.shape
    low = low_ref[...] + got_ref[:, got_ref.shape[1] - rank_most :].astype(f32)
    column = lax.broadcasted_iota(jnp.int32, (per_block, rank_most), 1)
    here_columns = slice(first, first + sum(widths))
    for start in range(0, total_rows, per_block):
        home, place, rank = block_place(table, start // per_block)
        here = slice(start, start + per_block)
        factor = adapter_alpha / rank.astype(f32)
        scaled = jnp.where(column < rank, low[here] * factor, 0.0).astype(bf16)
        for i in range(n_rep):

            @pl.when(home == i)
            def _():
                delta_ref[here, :] = jnp.dot(
                    scaled, ups[i][place, :, here_columns], preferred_element_type=f32
                )

    for start in range(0, total_rows, per_block):
        here = slice(start, start + per_block)
        at = 0
        for pairs, width in zip(addends, widths):
            there = slice(at, at + width)
            total = sum(a[here, off : off + width].astype(f32) for a, off in pairs)
            total += delta_ref[here, there].astype(bf16).astype(f32)
            for r in range(per_block // steps):
                done_ref[start // steps + r, :, there] = total[r * steps : (r + 1) * steps].astype(bf16)
            at += width
    copy = pltpu.make_async_copy(done_ref, out_ref.at[:, :, here_columns], sem)
    copy.start()
    copy.wait()


def finish(finals, widths, first, low, got, ups, table, held_out, steps, columns, per_block):
    total, rank = low.shape
    wide = sum(widths)
    operands = [a for addends in finals for a, _ in addends] + [low, got, *ups]
    in_specs = [pl.BlockSpec(memory_space=pltpu.SMEM)] * len(table)
    in_specs += [pl.BlockSpec(memory_space=pltpu.VMEM)] * len(operands)
    aliases = {}
    if held_out is not None:
        aliases = {len(table) + len(operands): 0}
        operands.append(held_out)
        in_specs.append(pl.BlockSpec(memory_space=pl.ANY))
    return pl.pallas_call(
        functools.partial(
            finish_kernel,
            offsets=[[off for _, off in addends] for addends in finals],
            widths=widths,
            first=first,
            n_rep=len(ups),
            per_block=per_block,
            held=ups[0].shape[0],
        ),
        in_specs=in_specs,
        out_specs=pl.BlockSpec(memory_space=pl.ANY),
        out_shape=jax.ShapeDtypeStruct((total // steps, steps, columns), bf16),
        scratch_shapes=[
            pltpu.VMEM((total, wide), f32),
            pltpu.VMEM((total // steps, steps, wide), bf16),
            pltpu.SemaphoreType.DMA,
        ],
        input_output_aliases=aliases,
        compiler_params=pltpu.CompilerParams(vmem_limit_bytes=12 << 20),
        cost_estimate=hint,
        name="finish",
    )(*map(in_hbm, table), *operands)


def halving_order(n):
    if n == 1:
        return [0]
    rest = halving_order(n // 2)
    return [2 * u + 1 for u in rest] + [2 * u for u in rest]


def after(x, *others):
    return lax.optimization_barrier((x, *others))[0]


def on_device(
    queries,
    cached_key_store,
    cached_value_store,
    decode_step_keys,
    decode_step_values,
    request_cache_length,
    output_projection_weight,
    adapter_down_weight,
    adapter_up_weight,
    adapter_store_slot,
    adapter_ranks,
    request_block_adapter,
):
    n_tp, n_rep = lax.axis_size("tp"), lax.axis_size("rep")
    me = lax.axis_index("tp")[None].astype(jnp.int32)
    my_rep = lax.axis_index("rep")[None].astype(jnp.int32)
    reqs, steps, width = queries.shape
    blocks = request_block_adapter.shape[0]
    columns = width // n_tp
    per_block = reqs * n_tp * steps // blocks
    table = (my_rep, request_block_adapter, adapter_store_slot, adapter_ranks)

    arrays = (
        queries,
        cached_key_store,
        cached_value_store,
        decode_step_keys,
        decode_step_values,
        request_cache_length,
    )
    order = halving_order(n_tp)
    eighth = columns // 8
    widths = [4 * eighth, 3 * eighth, 1 * eighth] if eighth % lanes == 0 else [columns // 2] * 2
    parts = len(widths)
    starts = [sum(widths[:q]) for q in range(parts)]
    owners = n_tp // 2
    top_bit = n_rep // 2

    def relay(x, across, go):
        held = {0: after(x, go), top_bit: after(across, go)}
        bit = top_bit // 2
        while bit >= 1:
            for p in list(held):
                held[p ^ bit] = swap(held[p], "rep", bit)
            bit //= 2
        return [held[p] for p in range(n_rep)]

    far, near = range(1, n_tp), range(1)
    own = dict(zip(far, attend(*arrays, me, far, n_tp)))
    pieces = {p: swap(own[p], "tp", p) for p in reversed(far)}
    own.update(zip(near, attend(*arrays, me, near, n_tp, [own[n_tp - 1]])))
    pieces[0] = own[0]
    down_across = swap(after(adapter_down_weight, own[0]), "rep", top_bit)
    weight = load(output_projection_weight, me, order[:owners], widths[0], columns, [own[0]])

    send, x = project([pieces[p] for p in range(n_tp)], weight, me)
    *sends, keep = project_rest(x, output_projection_weight, me, order, widths, columns)
    up_across = swap(after(adapter_up_weight, keep), "rep", top_bit)
    gots = [swap(send, "tp", 1) for send in (send, *sends)]
    finals, last = [], []
    low = None
    for q in range(parts):
        if q == parts - 1:
            send, low = project_last(
                x,
                output_projection_weight,
                downs,
                me,
                table,
                order[:owners],
                widths[q],
                columns,
                per_block,
                last,
            )
            gots.append(swap(send, "tp", 1))
        addends = [(keep, owners * starts[q]), (gots[q], 0)]
        wide = owners * widths[q]
        bit = 2
        while bit < n_tp:
            wide //= 2
            first = bit == 2
            waits = last + ([up_across] if q == 1 else []) + ([finals[q - 2][-1][0]] if q >= 2 else [])
            out = combine(addends, wide, low, waits if first else [])
            if first:
                last = [out[0]]
            if low is not None:
                low = out[1]
            got = swap(out[0], "tp", bit)
            addends = [(a, off + wide) for a, off in addends] + [(got, 0)]
            bit *= 2
        finals.append(addends)
        if q == 0:
            downs = relay(adapter_down_weight, down_across, last[0])
        if q == 1:
            ups = relay(adapter_up_weight, up_across, last[0])
    return finish(finals, widths, 0, low, got, ups, table, None, steps, columns, per_block)


def solution(mesh):
    placed = (
        P(("parts", "rep", "tp"), None, None),
        P(("parts", "rep", "tp"), None, None, None),
        P(("parts", "rep", "tp"), None, None, None),
        P(("parts", "rep", "tp"), None, None, None),
        P(("parts", "rep", "tp"), None, None, None),
        P(("parts", "rep", "tp")),
        P("tp", None),
        P("rep", "tp", None),
        P("rep", None, "tp"),
        P(),
        P(),
        P("rep"),
    )
    return jax.shard_map(
        on_device,
        mesh=mesh,
        in_specs=placed,
        out_specs=P(("parts", "rep"), None, "tp"),
        check_vma=False,
    )
```

```python
import functools
import math

import jax
import jax.numpy as jnp
from jax import lax
from jax.experimental import pallas as pl
from jax.experimental.pallas import tpu as pltpu
from jax.sharding import PartitionSpec as P

adapter_alpha = 16.0
lanes = 128
f32 = jnp.float32
bf16 = jnp.bfloat16
hint = pl.CostEstimate(flops=1, bytes_accessed=1, transcendentals=0)
long = pl.CostEstimate(flops=10**11, bytes_accessed=10**9, transcendentals=0)
mid = pl.CostEstimate(flops=8 * 10**9, bytes_accessed=8 * 10**6, transcendentals=0)


def swap(x, axis, bit):
    n = lax.axis_size(axis)
    return lax.ppermute(x, axis, [(i, i ^ bit) for i in range(n)])


def in_hbm(x):
    return pltpu.with_memory_space_constraint(x, pltpu.HBM)


def in_vmem(x):
    return pltpu.with_memory_space_constraint(x, pltpu.VMEM)


def attend_kernel(me_ref, len_ref, q_ref, dk_ref, dv_ref, *refs, pieces, n_tp, kv_count):
    count = len(pieces)
    k_refs, v_refs, outs = refs[:count], refs[count : 2 * count], refs[-count:]
    reqs, steps, width = q_ref.shape
    cache_len, head = k_refs[0].shape[2:]
    heads_each = width // head // n_tp
    group = width // head // kv_count
    feats = heads_each * head
    rows = heads_each * steps
    me = me_ref[0]
    scale = math.log2(math.e) / math.sqrt(head)
    fresh = steps * kv_count
    shape = (count * rows, lanes)
    row = lax.broadcasted_iota(jnp.int32, shape, 0)
    col = lax.broadcasted_iota(jnp.int32, shape, 1)
    row_kv = jnp.zeros(shape, jnp.int32)
    for u, p in enumerate(pieces):
        row_kv = jnp.where(row // rows == u, (me ^ p) * heads_each // group, row_kv)
    visible = (col % kv_count == row_kv) & (col // kv_count <= row % steps) & (col < fresh)
    base = pl.program_id(0) * reqs
    contract = (((1,), (1,)), ((), ()))
    pad = jnp.zeros((lanes - fresh, head), f32)

    def steps_of(ref, r):
        return jnp.concatenate([ref[r, t].astype(f32) for t in range(steps)] + [pad], axis=0).astype(bf16)

    old, new = [], []
    for r in range(reqs):
        parts = []
        for p in pieces:
            for g in range(heads_each):
                at = pl.multiple_of((me ^ p) * feats + g * head, lanes)
                parts.append(q_ref[r, :, pl.ds(at, head)].astype(f32))
        query = jnp.concatenate(parts, axis=0).astype(bf16)
        old.append(
            jnp.concatenate(
                [
                    lax.dot_general(
                        query[u * rows : (u + 1) * rows], k_refs[u][r, 0], contract, preferred_element_type=f32
                    )
                    for u in range(count)
                ],
                axis=0,
            )
        )
        new.append(lax.dot_general(query, steps_of(dk_ref, r), contract, preferred_element_type=f32))
    share, old_weight, new_weight = [], [], []
    for r in range(reqs):
        a = jnp.where(col < len_ref[base + r], old[r], -jnp.inf)
        b = jnp.where(visible, new[r], -jnp.inf)
        top = jnp.max(jnp.maximum(a, b), -1, keepdims=True)
        a = jnp.exp2((a - top) * scale)
        b = jnp.exp2((b - top) * scale)
        share.append(1.0 / jnp.sum(a + b, -1, keepdims=True))
        old_weight.append(a.astype(bf16))
        new_weight.append(b.astype(bf16))
    mixed = []
    for r in range(reqs):
        o = jnp.concatenate(
            [
                jnp.dot(old_weight[r][u * rows : (u + 1) * rows], v_refs[u][r, 0], preferred_element_type=f32)
                for u in range(count)
            ],
            axis=0,
        )
        o += jnp.dot(new_weight[r], steps_of(dv_ref, r), preferred_element_type=f32)
        mixed.append(o * share[r])
    for u in range(count):
        for g in range(heads_each):
            at = u * rows + g * steps
            stacked = jnp.concatenate([o[at : at + steps] for o in mixed], axis=0)
            outs[u][:, g * head : (g + 1) * head] = stacked.astype(bf16)


def attend(q, keys, values, new_keys, new_values, lengths, me, pieces, n_tp, waits=()):
    count, steps, width = q.shape
    kv_count, cache_len, head = keys.shape[1:]
    heads_each = width // head // n_tp
    group = width // head // kv_count
    assert group % heads_each == 0
    reqs = min(count, 8)
    feats = width // n_tp

    def cache_spec(p):
        return pl.BlockSpec(
            (reqs, 1, cache_len, head), lambda i, me, *_: (i, (me[0] ^ p) * heads_each // group, 0, 0)
        )

    q, keys, values, new_keys, new_values, lengths = map(
        in_hbm, (q, keys, values, new_keys, new_values, lengths)
    )
    return pl.pallas_call(
        functools.partial(attend_kernel, pieces=pieces, n_tp=n_tp, kv_count=kv_count),
        grid_spec=pltpu.PrefetchScalarGridSpec(
            num_scalar_prefetch=2,
            grid=(count // reqs,),
            in_specs=[
                pl.BlockSpec((reqs, steps, width), lambda i, *_: (i, 0, 0)),
                pl.BlockSpec((reqs, steps, kv_count, head), lambda i, *_: (i, 0, 0, 0)),
                pl.BlockSpec((reqs, steps, kv_count, head), lambda i, *_: (i, 0, 0, 0)),
            ]
            + [cache_spec(p) for p in pieces] * 2
            + [pl.BlockSpec(memory_space=pl.ANY)] * len(waits),
            out_specs=[pl.BlockSpec((reqs * steps, feats), lambda i, *_: (i, 0))] * len(pieces),
        ),
        out_shape=[jax.ShapeDtypeStruct((count * steps, feats), bf16)] * len(pieces),
        compiler_params=pltpu.CompilerParams(vmem_limit_bytes=32 << 20),
        cost_estimate=hint,
        name="attention",
    )(me, lengths, q, new_keys, new_values, *([keys] * len(pieces)), *([values] * len(pieces)), *waits)


def weight_copies(me, w_ref, out, sems, owners, columns, start, width):
    copies = []
    for u, p in enumerate(owners):
        at = pl.multiple_of((me ^ p) * columns + start, lanes)
        copies.append(
            pltpu.make_async_copy(
                w_ref.at[:, pl.ds(at, width)], out.at[:, u * width : (u + 1) * width], sems.at[u]
            )
        )
    return copies


def load_kernel(me_ref, w_ref, *refs, owners, part, columns):
    out_ref, sems = refs[-2:]
    copies = weight_copies(me_ref[0], w_ref, out_ref, sems, owners, columns, 0, part)
    for copy in copies:
        copy.start()
    for copy in copies:
        copy.wait()


def load(weight, me, owners, part, columns, waits):
    return pl.pallas_call(
        functools.partial(load_kernel, owners=owners, part=part, columns=columns),
        in_specs=[pl.BlockSpec(memory_space=pltpu.SMEM)]
        + [pl.BlockSpec(memory_space=pl.ANY)] * (1 + len(waits)),
        out_specs=pl.BlockSpec(memory_space=pltpu.VMEM),
        out_shape=pltpu.VMEM((weight.shape[0], len(owners) * part), weight.dtype),
        scratch_shapes=[pltpu.SemaphoreType.DMA((len(owners),))],
        compiler_params=pltpu.CompilerParams(vmem_limit_bytes=8 << 20),
        cost_estimate=hint,
        name="load",
    )(me, in_hbm(weight), *waits)


def block_place(table, b):
    rep_ref, adapter_ref, slot_ref, rank_ref, held = table
    adapter = adapter_ref[b]
    slot = slot_ref[adapter]
    return (slot // held) ^ rep_ref[0], slot % held, rank_ref[adapter]


def gather_kernel(me_ref, *refs, places):
    *pieces, x_ref = refs
    rows = pieces[0].shape[0]
    for p, piece in zip(places, pieces):
        x_ref[pl.ds(pl.multiple_of((me_ref[0] ^ p) * rows, rows), rows), :] = piece[...]


def gather(pieces, n_tp, me):
    places = list(pieces)
    rows, feats = pieces[places[0]].shape
    vmem = pl.BlockSpec(memory_space=pltpu.VMEM)
    return pl.pallas_call(
        functools.partial(gather_kernel, places=places),
        in_specs=[pl.BlockSpec(memory_space=pltpu.SMEM)] + [vmem] * len(places),
        out_specs=vmem,
        out_shape=jax.ShapeDtypeStruct((rows * n_tp, feats), bf16),
        compiler_params=pltpu.CompilerParams(vmem_limit_bytes=8 << 20),
        cost_estimate=long,
        name="gather",
    )(me, *(pieces[p] for p in places))


def project_kernel(me_ref, piece_ref, w_ref, _, out_ref, x_ref, *, place):
    rows = piece_ref.shape[0]
    x_ref[pl.ds(pl.multiple_of((me_ref[0] ^ place) * rows, rows), rows), :] = piece_ref[...]
    out_ref[...] = jnp.dot(x_ref[...], w_ref[...], preferred_element_type=f32).astype(bf16)


def project(x, piece, place, weight, me):
    vmem = pl.BlockSpec(memory_space=pltpu.VMEM)
    return pl.pallas_call(
        functools.partial(project_kernel, place=place),
        in_specs=[pl.BlockSpec(memory_space=pltpu.SMEM)] + [vmem] * 3,
        out_specs=[vmem] * 2,
        out_shape=[
            jax.ShapeDtypeStruct((x.shape[0], weight.shape[1]), bf16),
            jax.ShapeDtypeStruct(x.shape, bf16),
        ],
        input_output_aliases={3: 1},
        compiler_params=pltpu.CompilerParams(vmem_limit_bytes=12 << 20),
        cost_estimate=long,
        name="projection",
    )(me, piece, in_vmem(weight), x)


def project_rest_kernel(me_ref, x_ref, w_ref, *refs, order, widths, columns):
    parts, owners = len(widths), len(order) // 2
    outs, keep_ref = refs[: parts - 2], refs[parts - 2]
    nears, sems = refs[parts - 1 : -1], refs[-1]
    starts = [sum(widths[:q]) for q in range(parts)]
    jobs = [(order[:owners], q) for q in range(1, parts - 1)] + [(order[owners:], q) for q in range(parts)]
    copies = [
        weight_copies(me_ref[0], w_ref, near, sems.at[h], relative, columns, starts[q], widths[q])
        for h, (near, (relative, q)) in enumerate(zip(nears, jobs))
    ]
    for group in copies:
        for copy in group:
            copy.start()
    for h, (near, (_, q)) in enumerate(zip(nears, jobs)):
        for copy in copies[h]:
            copy.wait()
        got = jnp.dot(x_ref[...], near[...], preferred_element_type=f32).astype(bf16)
        if h < parts - 2:
            outs[h][...] = got
        else:
            keep_ref[:, owners * starts[q] : owners * (starts[q] + widths[q])] = got


def project_rest(x, weight, me, order, widths, columns):
    rows, feats = x.shape
    parts, owners = len(widths), len(order) // 2
    vmem = pl.BlockSpec(memory_space=pltpu.VMEM)
    return pl.pallas_call(
        functools.partial(project_rest_kernel, order=order, widths=widths, columns=columns),
        in_specs=[pl.BlockSpec(memory_space=pltpu.SMEM), vmem, pl.BlockSpec(memory_space=pl.ANY)],
        out_specs=[vmem] * (parts - 1),
        out_shape=[jax.ShapeDtypeStruct((rows, owners * w), bf16) for w in (*widths[1:-1], columns)],
        scratch_shapes=[pltpu.VMEM((feats, owners * w), weight.dtype) for w in (*widths[1:-1], *widths)]
        + [pltpu.SemaphoreType.DMA((2 * parts - 2, owners))],
        compiler_params=pltpu.CompilerParams(vmem_limit_bytes=20 << 20),
        cost_estimate=hint,
        name="projection_rest",
    )(me, x, in_hbm(weight))


def project_last_kernel(me_ref, *refs, owners, width, columns, adapters, per_block, held, waits):
    table, refs = (*refs[:4], held), refs[4:]
    x_ref, w_ref, downs = refs[0], refs[1], refs[2 : 2 + adapters]
    out_ref, low_ref, near, sems = refs[2 + adapters + waits :]
    copies = weight_copies(me_ref[0], w_ref, near, sems, owners, columns, columns - width, width)
    for copy in copies:
        copy.start()
    wide = len(owners) * width
    for start in range(0, x_ref.shape[0], per_block):
        home, place, _ = block_place(table, start // per_block)
        here = slice(start, start + per_block)
        for i in range(adapters):

            @pl.when(home == i)
            def _():
                got = jnp.dot(x_ref[here, :], downs[i][place], preferred_element_type=f32)
                low_ref[here, :] = got
                out_ref[here, wide:] = got.astype(bf16)

    for copy in copies:
        copy.wait()
    out_ref[:, :wide] = jnp.dot(x_ref[...], near[...], preferred_element_type=f32).astype(bf16)


def project_last(x, weight, downs, me, table, owners, width, columns, per_block, waits):
    rows, feats = x.shape
    held, _, rank = downs[0].shape
    wide = len(owners) * width
    vmem = pl.BlockSpec(memory_space=pltpu.VMEM)
    return pl.pallas_call(
        functools.partial(
            project_last_kernel,
            owners=owners,
            width=width,
            columns=columns,
            adapters=len(downs),
            per_block=per_block,
            held=held,
            waits=len(waits),
        ),
        in_specs=[pl.BlockSpec(memory_space=pltpu.SMEM)] * (1 + len(table))
        + [vmem, pl.BlockSpec(memory_space=pl.ANY)]
        + [vmem] * len(downs)
        + [pl.BlockSpec(memory_space=pl.ANY)] * len(waits),
        out_specs=[vmem] * 2,
        out_shape=[
            jax.ShapeDtypeStruct((rows, wide + rank), bf16),
            jax.ShapeDtypeStruct((rows, rank), f32),
        ],
        scratch_shapes=[
            pltpu.VMEM((feats, wide), weight.dtype),
            pltpu.SemaphoreType.DMA((len(owners),)),
        ],
        compiler_params=pltpu.CompilerParams(vmem_limit_bytes=16 << 20),
        cost_estimate=hint,
        name="projection_last",
    )(me, *map(in_hbm, table), x, in_hbm(weight), *downs, *waits)


def combine_kernel(*refs, offsets, wide, with_low, waits):
    refs = refs[waits:]
    n = len(offsets)
    addends, refs = refs[:n], refs[n:]
    total = sum(a[:, off : off + wide].astype(f32) for a, off in zip(addends, offsets))
    if with_low:
        low_ref, send_ref, low_out_ref = refs
        low = low_ref[...] + addends[-1][:, addends[-1].shape[1] - lanes :].astype(f32)
        low_out_ref[...] = low
        send_ref[:, wide:] = low.astype(bf16)
    else:
        (send_ref,) = refs
    send_ref[:, :wide] = total.astype(bf16)


def combine(addends, wide, low, waits, cost):
    arrays = [a for a, _ in addends]
    rows = arrays[0].shape[0]
    rank = 0 if low is None else low.shape[1]
    out_shape = [jax.ShapeDtypeStruct((rows, wide + rank), bf16)]
    if low is not None:
        arrays.append(low)
        out_shape.append(jax.ShapeDtypeStruct((rows, rank), f32))
    return pl.pallas_call(
        functools.partial(
            combine_kernel,
            offsets=[off for _, off in addends],
            wide=wide,
            with_low=low is not None,
            waits=len(waits),
        ),
        in_specs=[pl.BlockSpec(memory_space=pl.ANY)] * len(waits)
        + [pl.BlockSpec(memory_space=pltpu.VMEM)] * len(arrays),
        out_specs=[pl.BlockSpec(memory_space=pltpu.VMEM)] * len(out_shape),
        out_shape=out_shape,
        compiler_params=pltpu.CompilerParams(vmem_limit_bytes=8 << 20),
        cost_estimate=cost,
        name="combine",
    )(*waits, *arrays)


def finish_kernel(*refs, offsets, widths, first, n_rep, per_block, held):
    table, refs = (*refs[:4], held), refs[4:]
    addends = []
    for part_offsets in offsets:
        addends.append(list(zip(refs, part_offsets)))
        refs = refs[len(part_offsets) :]
    low_ref, got_ref, refs = refs[0], refs[1], refs[2:]
    ups, refs = refs[:n_rep], refs[n_rep:]
    out_ref, delta_ref, done_ref, sem = refs[-4:]
    steps = out_ref.shape[1]
    total_rows, rank_most = low_ref.shape
    low = low_ref[...] + got_ref[:, got_ref.shape[1] - rank_most :].astype(f32)
    column = lax.broadcasted_iota(jnp.int32, (per_block, rank_most), 1)
    here_columns = slice(first, first + sum(widths))
    for start in range(0, total_rows, per_block):
        home, place, rank = block_place(table, start // per_block)
        here = slice(start, start + per_block)
        factor = adapter_alpha / rank.astype(f32)
        scaled = jnp.where(column < rank, low[here] * factor, 0.0).astype(bf16)
        for i in range(n_rep):

            @pl.when(home == i)
            def _():
                delta_ref[here, :] = jnp.dot(
                    scaled, ups[i][place, :, here_columns], preferred_element_type=f32
                )

    for start in range(0, total_rows, per_block):
        here = slice(start, start + per_block)
        at = 0
        for pairs, width in zip(addends, widths):
            there = slice(at, at + width)
            total = sum(a[here, off : off + width].astype(f32) for a, off in pairs)
            total += delta_ref[here, there].astype(bf16).astype(f32)
            for r in range(per_block // steps):
                done_ref[start // steps + r, :, there] = total[r * steps : (r + 1) * steps].astype(bf16)
            at += width
    copy = pltpu.make_async_copy(done_ref, out_ref.at[:, :, here_columns], sem)
    copy.start()
    copy.wait()


def finish(finals, widths, first, low, got, ups, table, held_out, steps, columns, per_block):
    total, rank = low.shape
    wide = sum(widths)
    operands = [a for addends in finals for a, _ in addends] + [low, got, *ups]
    in_specs = [pl.BlockSpec(memory_space=pltpu.SMEM)] * len(table)
    in_specs += [pl.BlockSpec(memory_space=pltpu.VMEM)] * len(operands)
    aliases = {}
    if held_out is not None:
        aliases = {len(table) + len(operands): 0}
        operands.append(held_out)
        in_specs.append(pl.BlockSpec(memory_space=pl.ANY))
    return pl.pallas_call(
        functools.partial(
            finish_kernel,
            offsets=[[off for _, off in addends] for addends in finals],
            widths=widths,
            first=first,
            n_rep=len(ups),
            per_block=per_block,
            held=ups[0].shape[0],
        ),
        in_specs=in_specs,
        out_specs=pl.BlockSpec(memory_space=pl.ANY),
        out_shape=jax.ShapeDtypeStruct((total // steps, steps, columns), bf16),
        scratch_shapes=[
            pltpu.VMEM((total, wide), f32),
            pltpu.VMEM((total // steps, steps, wide), bf16),
            pltpu.SemaphoreType.DMA,
        ],
        input_output_aliases=aliases,
        compiler_params=pltpu.CompilerParams(vmem_limit_bytes=12 << 20),
        cost_estimate=hint,
        name="finish",
    )(*map(in_hbm, table), *operands)


def halving_order(n):
    if n == 1:
        return [0]
    rest = halving_order(n // 2)
    return [2 * u + 1 for u in rest] + [2 * u for u in rest]


def after(x, *others):
    return lax.optimization_barrier((x, *others))[0]


def on_device(
    queries,
    cached_key_store,
    cached_value_store,
    decode_step_keys,
    decode_step_values,
    request_cache_length,
    output_projection_weight,
    adapter_down_weight,
    adapter_up_weight,
    adapter_store_slot,
    adapter_ranks,
    request_block_adapter,
):
    n_tp, n_rep = lax.axis_size("tp"), lax.axis_size("rep")
    me = lax.axis_index("tp")[None].astype(jnp.int32)
    my_rep = lax.axis_index("rep")[None].astype(jnp.int32)
    reqs, steps, width = queries.shape
    blocks = request_block_adapter.shape[0]
    columns = width // n_tp
    per_block = reqs * n_tp * steps // blocks
    table = (my_rep, request_block_adapter, adapter_store_slot, adapter_ranks)

    arrays = (
        queries,
        cached_key_store,
        cached_value_store,
        decode_step_keys,
        decode_step_values,
        request_cache_length,
    )
    order = halving_order(n_tp)
    eighth = columns // 8
    widths = [4 * eighth, 3 * eighth, 1 * eighth] if eighth % lanes == 0 else [columns // 2] * 2
    parts = len(widths)
    starts = [sum(widths[:q]) for q in range(parts)]
    owners = n_tp // 2
    top_bit = n_rep // 2

    def relay(x, across, go):
        held = {0: after(x, go), top_bit: after(across, go)}
        bit = top_bit // 2
        while bit >= 1:
            for p in list(held):
                held[p ^ bit] = swap(held[p], "rep", bit)
            bit //= 2
        return [held[p] for p in range(n_rep)]

    far, near = range(2, n_tp), range(2)
    own = dict(zip(far, attend(*arrays, me, far, n_tp)))
    pieces = {p: swap(own[p], "tp", p) for p in far}
    own.update(zip(near, attend(*arrays, me, near, n_tp, [own[n_tp - 1]])))
    piece = swap(own[1], "tp", 1)
    weight = load(output_projection_weight, me, order[:owners], widths[0], columns, [own[0]])
    down_across = swap(after(adapter_down_weight, weight), "rep", top_bit)

    send, x = project(gather({0: own[0], **pieces}, n_tp, me), piece, 1, weight, me)
    *sends, keep = project_rest(x, output_projection_weight, me, order, widths, columns)
    downs = relay(adapter_down_weight, down_across, keep)
    up_across = swap(after(adapter_up_weight, keep), "rep", top_bit)
    gots = [swap(send, "tp", 1) for send in (send, *sends)]
    finals, last = [], []
    for q in range(parts):
        addends = [(keep, owners * starts[q]), (gots[q], 0)]
        wide = owners * widths[q]
        bit = 2
        while bit < n_tp:
            wide //= 2
            first = bit == 2
            waits = last + ([up_across] if q == 1 else []) + ([finals[q - 2][-1][0]] if q >= 2 else [])
            out = combine(
                addends,
                wide,
                low if q == parts - 1 else None,
                waits if first else [],
                (long if q else mid) if first else hint,
            )
            if first:
                last = [out[0]]
            if q == parts - 1:
                low = out[1]
            got = swap(out[0], "tp", bit)
            addends = [(a, off + wide) for a, off in addends] + [(got, 0)]
            bit *= 2
        finals.append(addends)
        if q == 0:
            send, low = project_last(
                x,
                output_projection_weight,
                downs,
                me,
                table,
                order[:owners],
                widths[-1],
                columns,
                per_block,
                last,
            )
            gots.append(swap(send, "tp", 1))
        if q == 1:
            ups = relay(adapter_up_weight, up_across, last[0])
    return finish(finals, widths, 0, low, got, ups, table, None, steps, columns, per_block)


def solution(mesh):
    placed = (
        P(("parts", "rep", "tp"), None, None),
        P(("parts", "rep", "tp"), None, None, None),
        P(("parts", "rep", "tp"), None, None, None),
        P(("parts", "rep", "tp"), None, None, None),
        P(("parts", "rep", "tp"), None, None, None),
        P(("parts", "rep", "tp")),
        P("tp", None),
        P("rep", "tp", None),
        P("rep", None, "tp"),
        P(),
        P(),
        P("rep"),
    )
    return jax.shard_map(
        on_device,
        mesh=mesh,
        in_specs=placed,
        out_specs=P(("parts", "rep"), None, "tp"),
        check_vma=False,
    )
```

```python
import functools
import math

import jax
import jax.numpy as jnp
from jax import lax
from jax.experimental import pallas as pl
from jax.experimental.pallas import tpu as pltpu
from jax.sharding import PartitionSpec as P

adapter_alpha = 16.0
lanes = 128
f32 = jnp.float32
bf16 = jnp.bfloat16
hint = pl.CostEstimate(flops=1, bytes_accessed=1, transcendentals=0)
long = pl.CostEstimate(flops=10**11, bytes_accessed=10**9, transcendentals=0)
short = pl.CostEstimate(flops=10**9, bytes_accessed=10**6, transcendentals=0)
mid = pl.CostEstimate(flops=8 * 10**9, bytes_accessed=8 * 10**6, transcendentals=0)


def swap(x, axis, bit):
    n = lax.axis_size(axis)
    return lax.ppermute(x, axis, [(i, i ^ bit) for i in range(n)])


def in_hbm(x):
    return pltpu.with_memory_space_constraint(x, pltpu.HBM)


def in_vmem(x):
    return pltpu.with_memory_space_constraint(x, pltpu.VMEM)


def attend_kernel(me_ref, len_ref, q_ref, dk_ref, dv_ref, *refs, pieces, n_tp, kv_count):
    count = len(pieces)
    k_refs, v_refs, outs = refs[:count], refs[count : 2 * count], refs[-count:]
    reqs, steps, width = q_ref.shape
    cache_len, head = k_refs[0].shape[2:]
    heads_each = width // head // n_tp
    group = width // head // kv_count
    feats = heads_each * head
    rows = heads_each * steps
    me = me_ref[0]
    scale = math.log2(math.e) / math.sqrt(head)
    fresh = steps * kv_count
    shape = (count * rows, lanes)
    row = lax.broadcasted_iota(jnp.int32, shape, 0)
    col = lax.broadcasted_iota(jnp.int32, shape, 1)
    row_kv = jnp.zeros(shape, jnp.int32)
    for u, p in enumerate(pieces):
        row_kv = jnp.where(row // rows == u, (me ^ p) * heads_each // group, row_kv)
    visible = (col % kv_count == row_kv) & (col // kv_count <= row % steps) & (col < fresh)
    base = pl.program_id(0) * reqs
    contract = (((1,), (1,)), ((), ()))
    pad = jnp.zeros((lanes - fresh, head), f32)

    def steps_of(ref, r):
        return jnp.concatenate([ref[r, t].astype(f32) for t in range(steps)] + [pad], axis=0).astype(bf16)

    old, new = [], []
    for r in range(reqs):
        parts = []
        for p in pieces:
            for g in range(heads_each):
                at = pl.multiple_of((me ^ p) * feats + g * head, lanes)
                parts.append(q_ref[r, :, pl.ds(at, head)].astype(f32))
        query = jnp.concatenate(parts, axis=0).astype(bf16)
        old.append(
            jnp.concatenate(
                [
                    lax.dot_general(
                        query[u * rows : (u + 1) * rows], k_refs[u][r, 0], contract, preferred_element_type=f32
                    )
                    for u in range(count)
                ],
                axis=0,
            )
        )
        new.append(lax.dot_general(query, steps_of(dk_ref, r), contract, preferred_element_type=f32))
    share, old_weight, new_weight = [], [], []
    for r in range(reqs):
        a = jnp.where(col < len_ref[base + r], old[r], -jnp.inf)
        b = jnp.where(visible, new[r], -jnp.inf)
        top = jnp.max(jnp.maximum(a, b), -1, keepdims=True)
        a = jnp.exp2((a - top) * scale)
        b = jnp.exp2((b - top) * scale)
        share.append(1.0 / jnp.sum(a + b, -1, keepdims=True))
        old_weight.append(a.astype(bf16))
        new_weight.append(b.astype(bf16))
    mixed = []
    for r in range(reqs):
        o = jnp.concatenate(
            [
                jnp.dot(old_weight[r][u * rows : (u + 1) * rows], v_refs[u][r, 0], preferred_element_type=f32)
                for u in range(count)
            ],
            axis=0,
        )
        o += jnp.dot(new_weight[r], steps_of(dv_ref, r), preferred_element_type=f32)
        mixed.append(o * share[r])
    for u in range(count):
        for g in range(heads_each):
            at = u * rows + g * steps
            stacked = jnp.concatenate([o[at : at + steps] for o in mixed], axis=0)
            outs[u][:, g * head : (g + 1) * head] = stacked.astype(bf16)


def attend(q, keys, values, new_keys, new_values, lengths, me, pieces, n_tp, waits=()):
    count, steps, width = q.shape
    kv_count, cache_len, head = keys.shape[1:]
    heads_each = width // head // n_tp
    group = width // head // kv_count
    assert group % heads_each == 0
    reqs = min(count, 8)
    feats = width // n_tp

    def cache_spec(p):
        return pl.BlockSpec(
            (reqs, 1, cache_len, head), lambda i, me, *_: (i, (me[0] ^ p) * heads_each // group, 0, 0)
        )

    q, keys, values, new_keys, new_values, lengths = map(
        in_hbm, (q, keys, values, new_keys, new_values, lengths)
    )
    return pl.pallas_call(
        functools.partial(attend_kernel, pieces=pieces, n_tp=n_tp, kv_count=kv_count),
        grid_spec=pltpu.PrefetchScalarGridSpec(
            num_scalar_prefetch=2,
            grid=(count // reqs,),
            in_specs=[
                pl.BlockSpec((reqs, steps, width), lambda i, *_: (i, 0, 0)),
                pl.BlockSpec((reqs, steps, kv_count, head), lambda i, *_: (i, 0, 0, 0)),
                pl.BlockSpec((reqs, steps, kv_count, head), lambda i, *_: (i, 0, 0, 0)),
            ]
            + [cache_spec(p) for p in pieces] * 2
            + [pl.BlockSpec(memory_space=pl.ANY)] * len(waits),
            out_specs=[pl.BlockSpec((reqs * steps, feats), lambda i, *_: (i, 0))] * len(pieces),
        ),
        out_shape=[jax.ShapeDtypeStruct((count * steps, feats), bf16)] * len(pieces),
        compiler_params=pltpu.CompilerParams(vmem_limit_bytes=32 << 20),
        cost_estimate=hint,
        name="attention",
    )(me, lengths, q, new_keys, new_values, *([keys] * len(pieces)), *([values] * len(pieces)), *waits)


def weight_copies(me, w_ref, out, sems, owners, columns, start, width):
    copies = []
    for u, p in enumerate(owners):
        at = pl.multiple_of((me ^ p) * columns + start, lanes)
        copies.append(
            pltpu.make_async_copy(
                w_ref.at[:, pl.ds(at, width)], out.at[:, u * width : (u + 1) * width], sems.at[u]
            )
        )
    return copies


def load_kernel(me_ref, w_ref, *refs, owners, part, columns):
    out_ref, sems = refs[-2:]
    copies = weight_copies(me_ref[0], w_ref, out_ref, sems, owners, columns, 0, part)
    for copy in copies:
        copy.start()
    for copy in copies:
        copy.wait()


def load(weight, me, owners, part, columns, waits):
    return pl.pallas_call(
        functools.partial(load_kernel, owners=owners, part=part, columns=columns),
        in_specs=[pl.BlockSpec(memory_space=pltpu.SMEM)]
        + [pl.BlockSpec(memory_space=pl.ANY)] * (1 + len(waits)),
        out_specs=pl.BlockSpec(memory_space=pltpu.VMEM),
        out_shape=pltpu.VMEM((weight.shape[0], len(owners) * part), weight.dtype),
        scratch_shapes=[pltpu.SemaphoreType.DMA((len(owners),))],
        compiler_params=pltpu.CompilerParams(vmem_limit_bytes=8 << 20),
        cost_estimate=hint,
        name="load",
    )(me, in_hbm(weight), *waits)


def block_place(table, b):
    rep_ref, adapter_ref, slot_ref, rank_ref, held = table
    adapter = adapter_ref[b]
    slot = slot_ref[adapter]
    return (slot // held) ^ rep_ref[0], slot % held, rank_ref[adapter]


def gather_kernel(me_ref, *refs, places):
    *pieces, x_ref = refs
    rows = pieces[0].shape[0]
    for p, piece in zip(places, pieces):
        x_ref[pl.ds(pl.multiple_of((me_ref[0] ^ p) * rows, rows), rows), :] = piece[...]


def gather(pieces, n_tp, me):
    places = list(pieces)
    rows, feats = pieces[places[0]].shape
    vmem = pl.BlockSpec(memory_space=pltpu.VMEM)
    return pl.pallas_call(
        functools.partial(gather_kernel, places=places),
        in_specs=[pl.BlockSpec(memory_space=pltpu.SMEM)] + [vmem] * len(places),
        out_specs=vmem,
        out_shape=jax.ShapeDtypeStruct((rows * n_tp, feats), bf16),
        compiler_params=pltpu.CompilerParams(vmem_limit_bytes=8 << 20),
        cost_estimate=long,
        name="gather",
    )(me, *(pieces[p] for p in places))


def project_kernel(me_ref, piece_ref, w_ref, _, out_ref, x_ref, *, place):
    rows = piece_ref.shape[0]
    x_ref[pl.ds(pl.multiple_of((me_ref[0] ^ place) * rows, rows), rows), :] = piece_ref[...]
    out_ref[...] = jnp.dot(x_ref[...], w_ref[...], preferred_element_type=f32).astype(bf16)


def project(x, piece, place, weight, me):
    vmem = pl.BlockSpec(memory_space=pltpu.VMEM)
    return pl.pallas_call(
        functools.partial(project_kernel, place=place),
        in_specs=[pl.BlockSpec(memory_space=pltpu.SMEM)] + [vmem] * 3,
        out_specs=[vmem] * 2,
        out_shape=[
            jax.ShapeDtypeStruct((x.shape[0], weight.shape[1]), bf16),
            jax.ShapeDtypeStruct(x.shape, bf16),
        ],
        input_output_aliases={3: 1},
        compiler_params=pltpu.CompilerParams(vmem_limit_bytes=12 << 20),
        cost_estimate=long,
        name="projection",
    )(me, piece, in_vmem(weight), x)


def project_rest_kernel(me_ref, x_ref, w_ref, *refs, order, widths, columns):
    parts, owners = len(widths), len(order) // 2
    outs, keep_ref = refs[: parts - 2], refs[parts - 2]
    nears, sems = refs[parts - 1 : -1], refs[-1]
    starts = [sum(widths[:q]) for q in range(parts)]
    jobs = [(order[:owners], q) for q in range(1, parts - 1)] + [(order[owners:], q) for q in range(parts)]
    copies = [
        weight_copies(me_ref[0], w_ref, near, sems.at[h], relative, columns, starts[q], widths[q])
        for h, (near, (relative, q)) in enumerate(zip(nears, jobs))
    ]
    for group in copies:
        for copy in group:
            copy.start()
    for h, (near, (_, q)) in enumerate(zip(nears, jobs)):
        for copy in copies[h]:
            copy.wait()
        got = jnp.dot(x_ref[...], near[...], preferred_element_type=f32).astype(bf16)
        if h < parts - 2:
            outs[h][...] = got
        else:
            keep_ref[:, owners * starts[q] : owners * (starts[q] + widths[q])] = got


def project_rest(x, weight, me, order, widths, columns):
    rows, feats = x.shape
    parts, owners = len(widths), len(order) // 2
    vmem = pl.BlockSpec(memory_space=pltpu.VMEM)
    return pl.pallas_call(
        functools.partial(project_rest_kernel, order=order, widths=widths, columns=columns),
        in_specs=[pl.BlockSpec(memory_space=pltpu.SMEM), vmem, pl.BlockSpec(memory_space=pl.ANY)],
        out_specs=[vmem] * (parts - 1),
        out_shape=[jax.ShapeDtypeStruct((rows, owners * w), bf16) for w in (*widths[1:-1], columns)],
        scratch_shapes=[pltpu.VMEM((feats, owners * w), weight.dtype) for w in (*widths[1:-1], *widths)]
        + [pltpu.SemaphoreType.DMA((2 * parts - 2, owners))],
        compiler_params=pltpu.CompilerParams(vmem_limit_bytes=20 << 20),
        cost_estimate=hint,
        name="projection_rest",
    )(me, x, in_hbm(weight))


def project_last_kernel(me_ref, *refs, owners, width, columns, adapters, per_block, held, waits):
    table, refs = (*refs[:4], held), refs[4:]
    x_ref, w_ref, downs = refs[0], refs[1], refs[2 : 2 + adapters]
    out_ref, low_ref, near, sems = refs[2 + adapters + waits :]
    copies = weight_copies(me_ref[0], w_ref, near, sems, owners, columns, columns - width, width)
    for copy in copies:
        copy.start()
    wide = len(owners) * width
    for start in range(0, x_ref.shape[0], per_block):
        home, place, _ = block_place(table, start // per_block)
        here = slice(start, start + per_block)
        for i in range(adapters):

            @pl.when(home == i)
            def _():
                got = jnp.dot(x_ref[here, :], downs[i][place], preferred_element_type=f32)
                low_ref[here, :] = got
                out_ref[here, wide:] = got.astype(bf16)

    for copy in copies:
        copy.wait()
    out_ref[:, :wide] = jnp.dot(x_ref[...], near[...], preferred_element_type=f32).astype(bf16)


def project_last(x, weight, downs, me, table, owners, width, columns, per_block, waits):
    rows, feats = x.shape
    held, _, rank = downs[0].shape
    wide = len(owners) * width
    vmem = pl.BlockSpec(memory_space=pltpu.VMEM)
    return pl.pallas_call(
        functools.partial(
            project_last_kernel,
            owners=owners,
            width=width,
            columns=columns,
            adapters=len(downs),
            per_block=per_block,
            held=held,
            waits=len(waits),
        ),
        in_specs=[pl.BlockSpec(memory_space=pltpu.SMEM)] * (1 + len(table))
        + [vmem, pl.BlockSpec(memory_space=pl.ANY)]
        + [vmem] * len(downs)
        + [pl.BlockSpec(memory_space=pl.ANY)] * len(waits),
        out_specs=[vmem] * 2,
        out_shape=[
            jax.ShapeDtypeStruct((rows, wide + rank), bf16),
            jax.ShapeDtypeStruct((rows, rank), f32),
        ],
        scratch_shapes=[
            pltpu.VMEM((feats, wide), weight.dtype),
            pltpu.SemaphoreType.DMA((len(owners),)),
        ],
        compiler_params=pltpu.CompilerParams(vmem_limit_bytes=16 << 20),
        cost_estimate=hint,
        name="projection_last",
    )(me, *map(in_hbm, table), x, in_hbm(weight), *downs, *waits)


def combine_kernel(*refs, offsets, wide, with_low, waits):
    refs = refs[waits:]
    n = len(offsets)
    addends, refs = refs[:n], refs[n:]
    total = sum(a[:, off : off + wide].astype(f32) for a, off in zip(addends, offsets))
    if with_low:
        low_ref, send_ref, low_out_ref = refs
        low = low_ref[...] + addends[-1][:, addends[-1].shape[1] - lanes :].astype(f32)
        low_out_ref[...] = low
        send_ref[:, wide:] = low.astype(bf16)
    else:
        (send_ref,) = refs
    send_ref[:, :wide] = total.astype(bf16)


def combine(addends, wide, low, waits, cost):
    arrays = [a for a, _ in addends]
    rows = arrays[0].shape[0]
    rank = 0 if low is None else low.shape[1]
    out_shape = [jax.ShapeDtypeStruct((rows, wide + rank), bf16)]
    if low is not None:
        arrays.append(low)
        out_shape.append(jax.ShapeDtypeStruct((rows, rank), f32))
    return pl.pallas_call(
        functools.partial(
            combine_kernel,
            offsets=[off for _, off in addends],
            wide=wide,
            with_low=low is not None,
            waits=len(waits),
        ),
        in_specs=[pl.BlockSpec(memory_space=pl.ANY)] * len(waits)
        + [pl.BlockSpec(memory_space=pltpu.VMEM)] * len(arrays),
        out_specs=[pl.BlockSpec(memory_space=pltpu.VMEM)] * len(out_shape),
        out_shape=out_shape,
        compiler_params=pltpu.CompilerParams(vmem_limit_bytes=8 << 20),
        cost_estimate=cost,
        name="combine",
    )(*waits, *arrays)


def pick_kernel(*refs, n_rep, per_block, held):
    table, refs = (*refs[:4], held), refs[4:]
    ups, (up_ref, scale_ref) = refs[:n_rep], refs[n_rep:]
    column = lax.broadcasted_iota(jnp.int32, (per_block, scale_ref.shape[1]), 1)
    for b in range(up_ref.shape[0]):
        home, place, rank = block_place(table, b)
        factor = adapter_alpha / rank.astype(f32)
        scale_ref[b * per_block : (b + 1) * per_block, :] = jnp.where(column < rank, factor, 0.0)
        for i in range(n_rep):

            @pl.when(home == i)
            def _():
                up_ref[b] = ups[i][place]


def pick(ups, table, blocks, per_block):
    held, rank, columns = ups[0].shape
    vmem = pl.BlockSpec(memory_space=pltpu.VMEM)
    return pl.pallas_call(
        functools.partial(pick_kernel, n_rep=len(ups), per_block=per_block, held=held),
        in_specs=[pl.BlockSpec(memory_space=pltpu.SMEM)] * len(table) + [vmem] * len(ups),
        out_specs=[vmem] * 2,
        out_shape=[
            jax.ShapeDtypeStruct((blocks, rank, columns), bf16),
            jax.ShapeDtypeStruct((blocks * per_block, rank), f32),
        ],
        compiler_params=pltpu.CompilerParams(vmem_limit_bytes=12 << 20),
        cost_estimate=hint,
        name="pick",
    )(*map(in_hbm, table), *ups)


def add_up_kernel(*refs, offsets, widths):
    *refs, _, out_ref = refs
    at = 0
    for part_offsets, width in zip(offsets, widths):
        addends, refs = refs[: len(part_offsets)], refs[len(part_offsets) :]
        total = sum(a[:, off : off + width].astype(f32) for a, off in zip(addends, part_offsets))
        out_ref[:, at : at + width] = total
        at += width


def add_up(finals, widths, wait):
    arrays = [a for addends in finals for a, _ in addends]
    vmem = pl.BlockSpec(memory_space=pltpu.VMEM)
    return pl.pallas_call(
        functools.partial(
            add_up_kernel, offsets=[[off for _, off in addends] for addends in finals], widths=widths
        ),
        in_specs=[vmem] * len(arrays) + [pl.BlockSpec(memory_space=pl.ANY)],
        out_specs=vmem,
        out_shape=jax.ShapeDtypeStruct((arrays[0].shape[0], sum(widths)), f32),
        compiler_params=pltpu.CompilerParams(vmem_limit_bytes=12 << 20),
        cost_estimate=long,
        name="add_up",
    )(*arrays, wait)


def finish_kernel(base_ref, low_ref, got_ref, up_ref, scale_ref, *refs, offsets, per_block):
    *addends, out_ref, done_ref, sems = refs
    reqs, steps, columns = done_ref.shape
    blocks, rank, _ = up_ref.shape
    first = base_ref.shape[1]
    low = low_ref[...] + got_ref[:, got_ref.shape[1] - rank :].astype(f32)
    scaled = (low * scale_ref[...]).astype(bf16)
    deltas = [
        jnp.dot(scaled[b * per_block : (b + 1) * per_block], up_ref[b], preferred_element_type=f32)
        for b in range(blocks)
    ]
    copies = []
    for b in range(blocks):
        here = slice(b * per_block, (b + 1) * per_block)
        delta = deltas[b].astype(bf16).astype(f32)
        last = sum(a[here, off : off + columns - first].astype(f32) for a, off in zip(addends, offsets))
        for there, total in (
            (slice(0, first), base_ref[here, :] + delta[:, :first]),
            (slice(first, columns), last + delta[:, first:]),
        ):
            for r in range(per_block // steps):
                at = b * per_block // steps + r
                done_ref[at, :, there] = total[r * steps : (r + 1) * steps].astype(bf16)
        mine = pl.ds(b * reqs // blocks, reqs // blocks)
        copies.append(pltpu.make_async_copy(done_ref.at[mine], out_ref.at[mine], sems.at[b]))
        copies[-1].start()
    for copy in copies:
        copy.wait()


def finish(base, addends, low, got, up, scale, steps, columns, per_block):
    total = low.shape[0]
    shape = (total // steps, steps, columns)
    arrays = [base, low, got, up, scale, *(a for a, _ in addends)]
    return pl.pallas_call(
        functools.partial(finish_kernel, offsets=[off for _, off in addends], per_block=per_block),
        in_specs=[pl.BlockSpec(memory_space=pltpu.VMEM)] * len(arrays),
        out_specs=pl.BlockSpec(memory_space=pl.ANY),
        out_shape=jax.ShapeDtypeStruct(shape, bf16),
        scratch_shapes=[pltpu.VMEM(shape, bf16), pltpu.SemaphoreType.DMA((up.shape[0],))],
        compiler_params=pltpu.CompilerParams(vmem_limit_bytes=16 << 20),
        cost_estimate=hint,
        name="finish",
    )(*arrays)


def halving_order(n):
    if n == 1:
        return [0]
    rest = halving_order(n // 2)
    return [2 * u + 1 for u in rest] + [2 * u for u in rest]


def after(x, *others):
    return lax.optimization_barrier((x, *others))[0]


def on_device(
    queries,
    cached_key_store,
    cached_value_store,
    decode_step_keys,
    decode_step_values,
    request_cache_length,
    output_projection_weight,
    adapter_down_weight,
    adapter_up_weight,
    adapter_store_slot,
    adapter_ranks,
    request_block_adapter,
):
    n_tp, n_rep = lax.axis_size("tp"), lax.axis_size("rep")
    me = lax.axis_index("tp")[None].astype(jnp.int32)
    my_rep = lax.axis_index("rep")[None].astype(jnp.int32)
    reqs, steps, width = queries.shape
    blocks = request_block_adapter.shape[0]
    columns = width // n_tp
    per_block = reqs * n_tp * steps // blocks
    table = (my_rep, request_block_adapter, adapter_store_slot, adapter_ranks)

    arrays = (
        queries,
        cached_key_store,
        cached_value_store,
        decode_step_keys,
        decode_step_values,
        request_cache_length,
    )
    order = halving_order(n_tp)
    eighth = columns // 8
    widths = [4 * eighth, 3 * eighth, 1 * eighth] if eighth % lanes == 0 else [columns // 2] * 2
    parts = len(widths)
    starts = [sum(widths[:q]) for q in range(parts)]
    owners = n_tp // 2
    top_bit = n_rep // 2

    def relay(x, across, go):
        held = {0: after(x, go), top_bit: after(across, go)}
        bit = top_bit // 2
        while bit >= 1:
            for p in list(held):
                held[p ^ bit] = swap(held[p], "rep", bit)
            bit //= 2
        return [held[p] for p in range(n_rep)]

    far, near = range(2, n_tp), range(2)
    own = dict(zip(far, attend(*arrays, me, far, n_tp)))
    pieces = {p: swap(own[p], "tp", p) for p in far}
    own.update(zip(near, attend(*arrays, me, near, n_tp, [own[n_tp - 1]])))
    piece = swap(own[1], "tp", 1)
    weight = load(output_projection_weight, me, order[:owners], widths[0], columns, [own[0]])
    down_across = swap(after(adapter_down_weight, weight), "rep", top_bit)

    send, x = project(gather({0: own[0], **pieces}, n_tp, me), piece, 1, weight, me)
    *sends, keep = project_rest(x, output_projection_weight, me, order, widths, columns)
    downs = relay(adapter_down_weight, down_across, keep)
    up_across = swap(after(adapter_up_weight, keep), "rep", top_bit)
    gots = [swap(send, "tp", 1) for send in (send, *sends)]
    finals, last = [], []
    for q in range(parts):
        addends = [(keep, owners * starts[q]), (gots[q], 0)]
        wide = owners * widths[q]
        bit = 2
        while bit < n_tp:
            wide //= 2
            first = bit == 2
            waits = last + []
            out = combine(
                addends,
                wide,
                low if q == parts - 1 else None,
                waits if first else [],
                (mid, long, short)[q] if first else hint,
            )
            if first:
                last = [out[0]]
            if q == parts - 1:
                low = out[1]
            got = swap(out[0], "tp", bit)
            addends = [(a, off + wide) for a, off in addends] + [(got, 0)]
            bit *= 2
        finals.append(addends)
        if q == 0:
            send, low = project_last(
                x,
                output_projection_weight,
                downs,
                me,
                table,
                order[:owners],
                widths[-1],
                columns,
                per_block,
                last,
            )
            gots.append(swap(send, "tp", 1))
        if q == 0:
            ups = relay(adapter_up_weight, up_across, last[0])
    up, scale = pick(ups, table, blocks, per_block)
    base = add_up(finals[:-1], widths[:-1], up)
    return finish(base, finals[-1], low, got, up, scale, steps, columns, per_block)


def solution(mesh):
    placed = (
        P(("parts", "rep", "tp"), None, None),
        P(("parts", "rep", "tp"), None, None, None),
        P(("parts", "rep", "tp"), None, None, None),
        P(("parts", "rep", "tp"), None, None, None),
        P(("parts", "rep", "tp"), None, None, None),
        P(("parts", "rep", "tp")),
        P("tp", None),
        P("rep", "tp", None),
        P("rep", None, "tp"),
        P(),
        P(),
        P("rep"),
    )
    return jax.shard_map(
        on_device,
        mesh=mesh,
        in_specs=placed,
        out_specs=P(("parts", "rep"), None, "tp"),
        check_vma=False,
    )
```
